256 devices in a mesh: section: 2 (over z_lo), tok: 16 (over x, y), wid: 8 (over z_hi, core).
Axes of the slice: x: 4, y: 4, z: 8 (z_hi: 4, z_lo: 2; z = z_hi * 2 + z_lo), core: 2. Of those that a mesh axis runs over, the one named last changes fastest.
Arguments:
- hidden: bfloat16 [4096, 24576], P('wid', ('section', 'tok')), may hold values from -6 to 6
- resid: bfloat16 [4096, 12288], P('wid', ('section', 'tok')), may hold values from -8 to 8
- down_weight: bfloat16 [24576, 12288], P(('section', 'tok'), 'wid'), may hold values from -0.078125 to 0.078125
- down_bias: float32 [12288], P(('section', 'tok')), may hold values from -3 to 3
- norm_gain: float32 [12288], P('wid'), may hold values from 0.1 to 1.9
- norm_shift: float32 [12288], P('wid'), may hold values from -3 to 3
- query_weight: bfloat16 [12288, 12288], P('wid', ('section', 'tok')), may hold values from -0.109375 to 0.109375
- query_bias: float32 [12288], P('wid'), may hold values from -3 to 3
Outputs:
- stream: bfloat16 [4096, 12288], P('wid', ('section', 'tok'))
- query: bfloat16 [8, 512, 12288], P(None, ('section', 'tok'), 'wid')
The draws below stay inside these ranges and needn't reach their ends.
All inputs are finite; a program needn't handle non-finite values.
Results may differ from the reference program's by a relative error of at most 0.029.
Values may be sent and summed in bfloat16 or wider, within the bound.
A program may use at most 128 MiB of HBM per device.

```python
import jax
import jax.numpy as jnp
from jax import lax

D = 12288
FFW = 24576
TOKENS = 4096
N_SECTION = 2
N_TOK = 16
N_WID = 8


def draw_resid(key, part):
    key = jax.random.fold_in(key, 11)
    column = jnp.arange(D, dtype=jnp.float32) / (D - 1)
    col_scale = 0.5 * jnp.exp(column * jnp.log(4.0))
    base = jnp.clip(jax.random.normal(key, (TOKENS, D), jnp.float32), -4.0, 4.0)
    return (base * col_scale).astype(jnp.bfloat16)


def raised(drawn, key, source, target, blocks, factor):
    owner, partner = [(jnp.arange(drawn.shape[axis_at]) // (drawn.shape[axis_at] // blocks)).reshape([-1 if axis == axis_at else 1 for axis in range(drawn.ndim)]) for axis_at in (source, target)]
    chosen = jax.random.permutation(key, blocks)[partner]
    strong = (owner == chosen) | (owner == (partner + blocks // 2) % blocks)
    return jnp.where(strong, factor * drawn, drawn)


def steps_of(key, dims, cuts, smallest, largest):
    loudness, own = 1.0, jax.random.fold_in(key, 6)
    for dim, blocks in cuts:
        heights = jnp.exp(jax.random.uniform(jax.random.fold_in(own, dim), (blocks,), jnp.float32, smallest / len(cuts), largest / len(cuts)))
        loudness = loudness * jnp.repeat(heights, dims[dim] // blocks).reshape([-1 if axis == dim else 1 for axis in range(len(dims))])
    return loudness


def bell_draw(key, extent, scale, limit, cuts=(), held_as=jnp.bfloat16):
    array = scale * jax.random.normal(key, extent, jnp.float32)
    if cuts:
        array = array * steps_of(key, extent, cuts, -0.22, 0.18)
    return jnp.clip(array, -limit, limit).astype(held_as)


def heavy_noise(rng, extent, width, bound, cuts, heavy, held_as=jnp.bfloat16):
    entries = width * jax.random.normal(rng, extent, jnp.float32)
    if cuts:
        entries = entries * steps_of(rng, extent, cuts, -0.22, 0.18)
    return jnp.clip(raised(entries, jax.random.fold_in(rng, 3), *heavy), -bound, bound).astype(held_as)


def setup_inputs(seed: int = 0) -> dict:
    seeds = jax.random.split(jax.random.key(seed), 9)
    return {
        "hidden": bell_draw(seeds[0], (TOKENS, FFW), 1.0, 6.0, ((0, 8), (1, 32))),
        "resid": draw_resid(jax.random.fold_in(seeds[8], 71), 0),
        "down_weight": heavy_noise(seeds[2], (FFW, D), FFW ** -0.5, 0.078125, ((0, 32), (1, 8)), (0, 1, 32, 2.75)),
        "down_bias": bell_draw(seeds[3], (D,), 0.5, 3.0, ((0, 32),), jnp.float32),
        "norm_gain": jnp.clip(1.0 + 0.18 * jax.random.normal(seeds[4], (D,), jnp.float32), 0.1, 1.9),
        "norm_shift": bell_draw(seeds[5], (D,), 0.5, 3.0, ((0, 8),), jnp.float32),
        "query_weight": heavy_noise(seeds[6], (D, D), D ** -0.5, 0.109375, ((0, 8), (1, 32)), (0, 1, 32, 2.75)),
        "query_bias": bell_draw(seeds[7], (D,), 0.5, 3.0, ((0, 8),), jnp.float32),
    }


norm_eps = 1e-05

def grouped_product(inputs, weights, groups):
    group_width = inputs.shape[1] // groups

    def add_group(running, group_index):
        start_col = (group_index * group_width).astype(jnp.int32)
        cols = lax.dynamic_slice_in_dim(inputs, start_col, group_width, 1)
        rows = lax.dynamic_slice_in_dim(weights, start_col, group_width, 0)
        term = jnp.dot(cols, rows, preferred_element_type=jnp.float32)
        term = lax.optimization_barrier(term.astype(jnp.bfloat16)).astype(jnp.float32)
        return (running + term, None)
    initial = jnp.zeros((inputs.shape[0], weights.shape[1]), jnp.float32)
    running, unused = lax.scan(add_group, initial, jnp.arange(groups, dtype=jnp.int32))
    return running

def reference(hidden, resid, down_weight, down_bias, norm_gain, norm_shift, query_weight, query_bias):
    down = grouped_product(hidden, down_weight, N_SECTION * N_TOK)
    stream = (resid.astype(jnp.float32) + down + down_bias).astype(jnp.bfloat16)
    row_values = stream.astype(jnp.float32)
    row_mean = lax.optimization_barrier(jnp.mean(row_values, axis=-1, keepdims=True))
    centred = row_values - row_mean
    row_var = lax.optimization_barrier(jnp.mean(centred * centred, axis=-1, keepdims=True))
    normed = (centred * lax.rsqrt(row_var + norm_eps) * norm_gain + norm_shift).astype(jnp.bfloat16)
    query = (grouped_product(normed, query_weight, N_WID) + query_bias).astype(jnp.bfloat16)
    return (stream, query.reshape(N_WID, TOKENS // N_WID, D))
```

```python
import jax
import jax.numpy as jnp
from jax import lax
from jax.sharding import PartitionSpec as P

norm_eps = 1e-05
ST = ("section", "tok")


def per_device(
    hidden, resid, down_weight, down_bias, norm_gain, norm_shift, query_weight, query_bias
):
    wid_count = lax.axis_size("wid")
    st_count = lax.axis_size("section") * lax.axis_size("tok")
    wid_index = lax.axis_index("wid")
    width = norm_gain.shape[0]
    rows = resid.shape[0] // st_count
    resid_rows = lax.all_to_all(resid, ST, split_axis=0, concat_axis=1, tiled=True)
    resid_own = lax.all_to_all(resid_rows, "wid", split_axis=1, concat_axis=0, tiled=True)
    bias = lax.dynamic_slice_in_dim(
        lax.all_gather(down_bias, ST, axis=0, tiled=True), wid_index * width, width, 0
    )
    hidden_all = lax.all_gather(hidden, "wid", axis=0, tiled=True)
    down_terms = jnp.dot(hidden_all, down_weight, preferred_element_type=jnp.float32)
    down_terms = down_terms.astype(jnp.bfloat16).reshape(wid_count, st_count, rows, width)
    down_share = lax.psum_scatter(down_terms, ST, scatter_dimension=1, tiled=True)
    down_share = down_share.reshape(wid_count * rows, width).astype(jnp.float32)
    stream_own = (resid_own.astype(jnp.float32) + down_share + bias).astype(jnp.bfloat16)
    stream = lax.all_to_all(stream_own, "wid", split_axis=0, concat_axis=1, tiled=True)
    stream = lax.all_to_all(stream, ST, split_axis=1, concat_axis=0, tiled=True)
    values = stream_own.astype(jnp.float32)
    own_mean = jnp.mean(values, axis=-1, keepdims=True)
    own_m2 = jnp.sum((values - own_mean) ** 2, axis=-1, keepdims=True)
    parts = lax.all_gather(jnp.concatenate([own_mean, own_m2], axis=1), "wid")
    row_mean = jnp.mean(parts[:, :, :1], axis=0)
    row_var = (
        jnp.sum(parts[:, :, 1:], axis=0) + width * jnp.sum((parts[:, :, :1] - row_mean) ** 2, axis=0)
    ) / (width * wid_count)
    normed = ((values - row_mean) * lax.rsqrt(row_var + norm_eps) * norm_gain + norm_shift).astype(
        jnp.bfloat16
    )
    normed_all = lax.all_gather(normed, ST, axis=0, tiled=True)
    query_terms = jnp.dot(normed_all, query_weight, preferred_element_type=jnp.float32)
    query_terms = query_terms.astype(jnp.bfloat16).reshape(st_count, wid_count, rows, -1)
    share = lax.psum_scatter(query_terms, "wid", scatter_dimension=1, tiled=True)
    share = share.reshape(st_count * rows, -1)
    share = lax.all_to_all(share, ST, split_axis=0, concat_axis=1, tiled=True)
    share = lax.all_to_all(share, "wid", split_axis=1, concat_axis=0, tiled=True)
    query = (share.astype(jnp.float32) + query_bias).astype(jnp.bfloat16)
    return (stream, query.reshape(wid_count, rows, width))


def solution(mesh):
    return jax.shard_map(
        per_device,
        mesh=mesh,
        in_specs=(
            P("wid", ST),
            P("wid", ST),
            P(ST, "wid"),
            P(ST),
            P("wid"),
            P("wid"),
            P("wid", ST),
            P("wid"),
        ),
        out_specs=(P("wid", ST), P(None, ST, "wid")),
        check_vma=False,
    )
```

```python
import functools

import jax
import jax.numpy as jnp
from jax import lax
from jax.experimental import pallas as pl
from jax.experimental.pallas import tpu as pltpu
from jax.sharding import PartitionSpec as P

norm_eps = 1e-05
ST = ("section", "tok")
F32, BF16 = jnp.float32, jnp.bfloat16
MESH = pl.DeviceIdType.MESH
UNITS = 16
LAG = 2


def add(*terms):
    total = terms[0].astype(F32)
    for term in terms[1:]:
        total = total + term.astype(F32)
    return total


def place():
    zlo, tok, wid = (lax.axis_index(name) for name in ("section", "tok", "wid"))
    return zlo, tok // 4, tok % 4, wid // 2, wid % 2


def down_kernel(
    hidden, resid, bias, weight, out,
    hbuf, rsrc, rbuf, pbuf, r1, r2, r3, r4, zs, zr, acc,
    own_sem, ag_send, ag_recv, res_send, res_recv, rs_send, rs_recv,
):
    zlo, x, y, zhi, c = place()
    tok, wid = x * 4 + y, zhi * 2 + c
    half = hbuf.shape[3]
    wide = weight.shape[1] // 2
    first, second = (x, y), (y, x)
    x_devs = [{"tok": (x + 1) % 4 * 4 + y}, {"tok": (x + 3) % 4 * 4 + y}]
    y_devs = [{"tok": x * 4 + (y + 1) % 4}, {"tok": x * 4 + (y + 3) % 4}]
    first_devs, second_devs = (x_devs, y_devs), (y_devs, x_devs)
    z_devs = [{"wid": (zhi + 1) % 4 * 2 + c}, {"wid": (zhi + 3) % 4 * 2 + c}]
    mate, pair = {"wid": zhi * 2 + 1 - c}, {"section": 1 - zlo}

    def remote(src, dst, send, recv, dev):
        return pltpu.make_async_remote_copy(src, dst, send, recv, device_id=dev, device_id_type=MESH)

    res_zhi, res_c, res_zlo, res_j = zlo * 2 + x // 2, x % 2, y // 2, y % 2
    res_wid = res_zhi * 2 + res_c
    res_self = jnp.logical_and(res_wid == wid, res_zlo == zlo)
    source = 4 * wid + 2 * zlo

    barrier = pltpu.get_barrier_semaphore()
    for dev in (*x_devs, *y_devs, *z_devs, mate, pair):
        pl.semaphore_signal(barrier, inc=1, device_id=dev, device_id_type=MESH)

    def greet(n, carry):
        group = source + n // 8
        is_self = jnp.logical_and(group == zlo * 16 + tok, n % 8 == wid)

        @pl.when(jnp.logical_not(is_self))
        def _():
            pl.semaphore_signal(
                barrier, inc=1, device_id=(group // 16, group % 16, n % 8), device_id_type=MESH
            )
        return carry

    lax.fori_loop(0, 16, greet, 0)

    @pl.when(res_self)
    def _():
        pl.semaphore_wait(barrier, 23)

    @pl.when(jnp.logical_not(res_self))
    def _():
        pl.semaphore_wait(barrier, 24)

    own_copy = pltpu.make_async_copy(hidden, hbuf.at[wid], own_sem)
    own_copy.start()

    def own_send(n):
        h = n % 2
        dev = (mate, *z_devs)[n // 2]
        step = (2 + h, 4 + 4 * h, 5 + 4 * h)[n // 2]
        return remote(hidden.at[h], hbuf.at[wid, h], ag_send.at[n], ag_recv.at[step], dev)

    for n in (2, 4, 0, 3, 5, 1):
        own_send(n).start()

    def block(i):
        g, k = i // 4, i % 4
        mid = (g + 1) // 2 % 2
        off = mid * (3 - 2 * (k % 2)) + 2 * (g // 3)
        h = mid * (g - 1) + (1 - mid) * (k % 2)
        return (zhi + off) % 4 * 2 + (c + k // 2) % 2, h

    def mate_send(i):
        w, h = block(i)
        return remote(hbuf.at[w, h], hbuf.at[w, h], ag_send.at[8 + i], ag_recv.at[i + 2], mate)

    def far_send(i, n):
        w, h = block(i)
        return remote(hbuf.at[w, h], hbuf.at[w, h], ag_send.at[6 + n], ag_recv.at[12 + n], z_devs[n])

    rsrc[...] = (resid[...].astype(F32) + bias[...].reshape(1, 1, 1, -1)).astype(BF16)
    narrow = resid.shape[3]

    def res_copy(n, local):
        src = rsrc.at[:, n]
        dst = rbuf.at[:, wid, :, pl.ds(pl.multiple_of(res_j * narrow, narrow), narrow)]
        if local:
            return pltpu.make_async_copy(src, dst, res_recv)
        return remote(src, dst, res_send.at[n], res_recv, (res_zlo, n, res_wid))

    def res_each(n, carry):
        is_self = jnp.logical_and(res_self, n == tok)

        @pl.when(is_self)
        def _():
            res_copy(n, True).start()

        @pl.when(jnp.logical_not(is_self))
        def _():
            res_copy(n, False).start()
        return carry

    lax.fori_loop(0, 16, res_each, 0)

    def chunk1(i, a, d, start, size):
        cols = pl.ds(a * wide, wide)
        if a == 0:
            return pbuf.at[i, d, pl.ds(start, size), :, cols]
        return pbuf.at[i, pl.ds(start, size), d, :, cols]

    def chunk2(i, a, d, start, size):
        cols = pl.ds(a * wide + start, size)
        if a == 0:
            return pbuf.at[i, x, d, :, cols]
        return pbuf.at[i, d, y, :, cols]

    def hop(i, a, s, n):
        sems = rs_send.at[i, a, s, n], rs_recv.at[i, a, s, n]
        near = (1, 3)[n]
        if s == 0:
            return remote(chunk1(i, a, (first[a] + 2) % 4, 2 * n, 2), r1.at[a, i, n], *sems, first_devs[a][n])
        if s == 1:
            return remote(chunk1(i, a, (first[a] + near) % 4, 0, 4), r2.at[a, i, n], *sems, first_devs[a][n])
        if s == 2:
            src = chunk2(i, a, (second[a] + 2) % 4, n * wide // 2, wide // 2)
            return remote(src, r3.at[a, i, n], *sems, second_devs[a][n])
        return remote(chunk2(i, a, (second[a] + near) % 4, 0, wide), r4.at[a, i, n], *sems, second_devs[a][n])

    def pair_hop(i):
        return remote(zs.at[i], zr.at[i], rs_send.at[i, 0, 4, 0], rs_recv.at[i, 0, 4, 0], pair)

    def multiply(i):
        w, h = block(i)

        @pl.when(i == 0)
        def _():
            own_copy.wait()

        @pl.when(i >= 2)
        def _():
            remote(hbuf.at[w, h], hbuf.at[w, h], ag_send.at[0], ag_recv.at[i], mate).wait_recv()

        @pl.when(i == 4)
        def _():
            far_send(i, 0).start()

        @pl.when(i == 9)
        def _():
            far_send(i, 1).start()

        @pl.when(jnp.logical_and(i >= 4, i % 4 < 2))
        def _():
            mate_send(i).start()

        rows = hbuf[w, h]
        for n in range(0, 2 * wide, 512):
            part = jnp.dot(rows, weight[:, n : n + 512], preferred_element_type=F32)
            pbuf[i, :, :, :, pl.ds(n, 512)] = part.astype(BF16).reshape(4, 4, 16, 512)
        for a in range(2):
            for n in range(2):
                hop(i, a, 0, n).start()

    def relay1(i):
        for a in range(2):
            for n in range(2):
                hop(i, a, 0, n).wait_recv()
                ref = chunk1(i, a, (first[a] + (1, 3)[n]) % 4, 2 * n, 2)
                ref[...] = add(ref[...], r1[a, i, n]).astype(BF16)
                hop(i, a, 1, n).start()

    def turn(i):
        for a in range(2):
            for n in range(2):
                hop(i, a, 1, n).wait_recv()
            ref = chunk1(i, a, first[a], 0, 4)
            ref[...] = add(ref[...], r2[a, i, 0], r2[a, i, 1]).astype(BF16)
            for n in range(2):
                hop(i, a, 2, n).start()

    def relay2(i):
        for a in range(2):
            for n in range(2):
                hop(i, a, 2, n).wait_recv()
                ref = chunk2(i, a, (second[a] + (1, 3)[n]) % 4, n * wide // 2, wide // 2)
                ref[...] = add(ref[...], r3[a, i, n]).astype(BF16)
                hop(i, a, 3, n).start()

    def plane_sum(i):
        for a in range(2):
            for n in range(2):
                hop(i, a, 3, n).wait_recv()
            total = add(chunk2(i, a, second[a], 0, wide)[...], r4[a, i, 0], r4[a, i, 1])

            @pl.when(zlo == a)
            def _():
                acc[i] = total

            @pl.when(zlo != a)
            def _():
                zs[i] = total.astype(BF16)
                pair_hop(i).start()

    def finish(i):
        w, h = block(i)

        @pl.when(i == 0)
        def _():
            pltpu.make_async_copy(rbuf, rbuf, res_recv).wait()

        pair_hop(i).wait_recv()
        out[h, w] = add(acc[i], zr[i], rbuf[h, w]).astype(BF16)

    stages = (multiply, relay1, turn, relay2, plane_sum, finish)

    def body(t, carry):
        for n in (0, 5, 4, 3, 2, 1):
            i = t - n * LAG

            @pl.when(jnp.logical_and(i >= 0, i < UNITS))
            def _():
                stages[n](i)
        return carry

    lax.fori_loop(0, UNITS + 5 * LAG, body, 0)

    for n in range(6):
        own_send(n).wait_send()
    for i in (4, 5, 8, 9, 12, 13):
        mate_send(i).wait_send()
    far_send(4, 0).wait_send()
    far_send(9, 1).wait_send()

    def res_done(n, carry):
        @pl.when(jnp.logical_not(jnp.logical_and(res_self, n == tok)))
        def _():
            res_copy(n, False).wait_send()
        return carry

    lax.fori_loop(0, 16, res_done, 0)

    def drain(i, carry):
        for a in range(2):
            for s in range(4):
                for n in range(2):
                    hop(i, a, s, n).wait_send()
        pair_hop(i).wait_send()
        return carry

    lax.fori_loop(0, UNITS, drain, 0)


def down(hidden, resid, bias, weight):
    rows, depth = hidden.shape
    width = weight.shape[1]
    wide = width // 2
    narrow = resid.shape[1]
    dma = pltpu.SemaphoreType.DMA
    return pl.pallas_call(
        down_kernel,
        out_shape=jax.ShapeDtypeStruct((2, 8, 16, wide), BF16),
        in_specs=[pl.BlockSpec(memory_space=pl.ANY)] + [pl.BlockSpec(memory_space=pltpu.VMEM)] * 3,
        out_specs=pl.BlockSpec(memory_space=pltpu.VMEM),
        scratch_shapes=[
            pltpu.VMEM((8, 2, rows // 2, depth), BF16),
            pltpu.VMEM((2, 16, 16, narrow), BF16),
            pltpu.VMEM((2, 8, 16, wide), BF16),
            pltpu.VMEM((UNITS, 4, 4, 16, width), BF16),
            pltpu.VMEM((2, UNITS, 2, 2, 16, wide), BF16),
            pltpu.VMEM((2, UNITS, 2, 4, 16, wide), BF16),
            pltpu.VMEM((2, UNITS, 2, 16, wide // 2), BF16),
            pltpu.VMEM((2, UNITS, 2, 16, wide), BF16),
            pltpu.VMEM((UNITS, 16, wide), BF16),
            pltpu.VMEM((UNITS, 16, wide), BF16),
            pltpu.VMEM((UNITS, 16, wide), F32),
            dma,
            dma((24,)),
            dma((16,)),
            dma((16,)),
            dma,
            dma((UNITS, 2, 5, 2)),
            dma((UNITS, 2, 5, 2)),
        ],
        compiler_params=pltpu.CompilerParams(
            collective_id=0, has_side_effects=True, vmem_limit_bytes=60 * 1024 * 1024
        ),
        cost_estimate=pl.CostEstimate(
            flops=2 * 8 * rows * depth * width, bytes_accessed=2 * (rows * depth + depth * width), transcendentals=0
        ),
    )(
        hidden.reshape(2, rows // 2, depth),
        resid.reshape(2, 16, 16, narrow),
        bias.reshape(1, narrow),
        weight,
    )


def per_device(
    hidden, resid, down_weight, down_bias, norm_gain, norm_shift, query_weight, query_bias
):
    wid_count = lax.axis_size("wid")
    st_count = lax.axis_size("section") * lax.axis_size("tok")
    wid_index = lax.axis_index("wid")
    width = norm_gain.shape[0]
    rows = resid.shape[0] // st_count
    down_out = down(hidden, resid, down_bias, down_weight)
    down_out = down_out.reshape(2, wid_count * rows, width // 2)
    stream_own = lax.all_to_all(down_out, "section", split_axis=0, concat_axis=2, tiled=True)
    stream_own = stream_own.reshape(wid_count * rows, width)
    stream = lax.all_to_all(stream_own, "wid", split_axis=0, concat_axis=1, tiled=True)
    stream = lax.all_to_all(stream, ST, split_axis=1, concat_axis=0, tiled=True)
    values = stream_own.astype(jnp.float32)
    own_mean = jnp.mean(values, axis=-1, keepdims=True)
    own_m2 = jnp.sum((values - own_mean) ** 2, axis=-1, keepdims=True)
    parts = lax.all_gather(jnp.concatenate([own_mean, own_m2], axis=1), "wid")
    row_mean = jnp.mean(parts[:, :, :1], axis=0)
    row_var = (
        jnp.sum(parts[:, :, 1:], axis=0) + width * jnp.sum((parts[:, :, :1] - row_mean) ** 2, axis=0)
    ) / (width * wid_count)
    normed = ((values - row_mean) * lax.rsqrt(row_var + norm_eps) * norm_gain + norm_shift).astype(
        jnp.bfloat16
    )
    normed_all = lax.all_gather(normed, ST, axis=0, tiled=True)
    query_terms = jnp.dot(normed_all, query_weight, preferred_element_type=jnp.float32)
    query_terms = query_terms.astype(jnp.bfloat16).reshape(st_count, wid_count, rows, -1)
    share = lax.psum_scatter(query_terms, "wid", scatter_dimension=1, tiled=True)
    share = share.reshape(st_count * rows, -1)
    share = lax.all_to_all(share, ST, split_axis=0, concat_axis=1, tiled=True)
    share = lax.all_to_all(share, "wid", split_axis=1, concat_axis=0, tiled=True)
    query = (share.astype(jnp.float32) + query_bias).astype(jnp.bfloat16)
    return (stream, query.reshape(wid_count, rows, width))


def solution(mesh):
    return jax.shard_map(
        per_device,
        mesh=mesh,
        in_specs=(
            P("wid", ST),
            P("wid", ST),
            P(ST, "wid"),
            P(ST),
            P("wid"),
            P("wid"),
            P("wid", ST),
            P("wid"),
        ),
        out_specs=(P("wid", ST), P(None, ST, "wid")),
        check_vma=False,
    )
```

```python
import functools

import jax
import jax.numpy as jnp
from jax import lax
from jax.experimental import pallas as pl
from jax.experimental.pallas import tpu as pltpu
from jax.sharding import PartitionSpec as P

norm_eps = 1e-05
ST = ("section", "tok")
F32, BF16 = jnp.float32, jnp.bfloat16
MESH = pl.DeviceIdType.MESH
UNITS = 16
LAG = 2
LAG2 = 2


def add(*terms):
    total = terms[0].astype(F32)
    for term in terms[1:]:
        total = total + term.astype(F32)
    return total


def place():
    zlo, tok, wid = (lax.axis_index(name) for name in ("section", "tok", "wid"))
    return zlo, tok // 4, tok % 4, wid // 2, wid % 2


def layer_kernel(
    hidden, resid, bias, weight, gain, shift, qweight, qbias, stream, query,
    hbuf, rsrc, rbuf, pbuf, r1, r2, r3, r4, zs, zr, acc,
    sbuf, stats, nbuf, qwm, bias2, cbuf, zbuf, fin,
    own_sem, ag_send, ag_recv, res_send, res_recv, rs_send, rs_recv,
    qw_sem, b_sem, st_send, st_recv, so_send, so_recv, n_send, n_recv,
    c_send, c_recv, z_send, z_recv, f_send, f_recv,
):
    zlo, x, y, zhi, c = place()
    tok, wid = x * 4 + y, zhi * 2 + c
    half = hbuf.shape[3]
    wide = weight.shape[1] // 2
    first, second = (x, y), (y, x)
    x_devs = [{"tok": (x + 1) % 4 * 4 + y}, {"tok": (x + 3) % 4 * 4 + y}]
    y_devs = [{"tok": x * 4 + (y + 1) % 4}, {"tok": x * 4 + (y + 3) % 4}]
    first_devs, second_devs = (x_devs, y_devs), (y_devs, x_devs)
    z_devs = [{"wid": (zhi + 1) % 4 * 2 + c}, {"wid": (zhi + 3) % 4 * 2 + c}]
    mate, pair = {"wid": zhi * 2 + 1 - c}, {"section": 1 - zlo}

    def remote(src, dst, send, recv, dev):
        return pltpu.make_async_remote_copy(src, dst, send, recv, device_id=dev, device_id_type=MESH)

    res_zhi, res_c, res_zlo, res_j = zlo * 2 + x // 2, x % 2, y // 2, y % 2
    res_wid = res_zhi * 2 + res_c
    res_self = jnp.logical_and(res_wid == wid, res_zlo == zlo)
    source = 4 * wid + 2 * zlo

    z = zhi * 2 + zlo
    me = z * 2 + c

    f_x, f_c = zhi % 2 * 2 + c, zhi // 2
    f_dest = zhi == 2 * c + x // 2
    f_self = jnp.logical_and(f_dest, c == x % 2)

    barrier = pltpu.get_barrier_semaphore()

    def greet(dev, unless=None):
        def go():
            pl.semaphore_signal(barrier, inc=1, device_id=dev, device_id_type=MESH)

        if unless is None:
            go()
        else:
            pl.when(jnp.logical_not(unless))(go)

    for dev in (*x_devs, *y_devs):
        greet(dev)

    def greet_each(n, carry):
        group = source + n // 8
        greet(
            (group // 16, group % 16, n % 8),
            jnp.logical_and(group == zlo * 16 + tok, n % 8 == wid),
        )
        greet((res_zlo, n, res_wid), jnp.logical_and(res_self, n == tok))
        greet((n // 2 % 2, tok, n // 4 * 2 + n % 2), n == me)
        return carry

    lax.fori_loop(0, 16, greet_each, 0)
    for n in range(4):
        greet(
            (zlo, f_x * 4 + n, zhi * 2 + f_c),
            jnp.logical_and(jnp.logical_and(f_x == x, f_c == c), n == y),
        )
    met = 4 + 32 + 15 - 2 * res_self.astype(jnp.int32)
    met = met + 16 * f_dest.astype(jnp.int32) - f_self.astype(jnp.int32)
    pl.semaphore_wait(barrier, met)

    own_copy = pltpu.make_async_copy(hidden, hbuf.at[wid], own_sem)
    own_copy.start()

    def own_send(n):
        h = n % 2
        dev = (mate, *z_devs)[n // 2]
        step = (2 + h, 4 + 4 * h, 5 + 4 * h)[n // 2]
        return remote(hidden.at[h], hbuf.at[wid, h], ag_send.at[n], ag_recv.at[step], dev)

    for n in (2, 4, 0, 3, 5, 1):
        own_send(n).start()

    bias2[c] = qbias[...]
    qw_own = pltpu.make_async_copy(qweight.at[zlo], qwm.at[zlo], qw_sem.at[0])
    qw_own.start()
    qw_pair = remote(qweight.at[1 - zlo], qwm.at[zlo], qw_sem.at[1], qw_sem.at[2], pair)
    bias_mate = remote(bias2.at[c], bias2.at[c], b_sem.at[0], b_sem.at[1], mate)
    bias_mate.start()

    def block(i):
        g, k = i // 4, i % 4
        mid = (g + 1) // 2 % 2
        off = mid * (3 - 2 * (k % 2)) + 2 * (g // 3)
        h = mid * (g - 1) + (1 - mid) * (k % 2)
        return (zhi + off) % 4 * 2 + (c + k // 2) % 2, h

    def mate_send(i):
        w, h = block(i)
        return remote(hbuf.at[w, h], hbuf.at[w, h], ag_send.at[8 + i], ag_recv.at[i + 2], mate)

    def far_send(i, n):
        w, h = block(i)
        return remote(hbuf.at[w, h], hbuf.at[w, h], ag_send.at[6 + n], ag_recv.at[12 + n], z_devs[n])

    rsrc[...] = (resid[...].astype(F32) + bias[...].reshape(1, 1, 1, -1)).astype(BF16)
    narrow = resid.shape[3]

    def res_copy(n, local):
        src = rsrc.at[:, n]
        dst = rbuf.at[:, wid, :, pl.ds(pl.multiple_of(res_j * narrow, narrow), narrow)]
        if local:
            return pltpu.make_async_copy(src, dst, res_recv)
        return remote(src, dst, res_send.at[n], res_recv, (res_zlo, n, res_wid))

    def res_each(n, carry):
        is_self = jnp.logical_and(res_self, n == tok)

        @pl.when(is_self)
        def _():
            res_copy(n, True).start()

        @pl.when(jnp.logical_not(is_self))
        def _():
            res_copy(n, False).start()
        return carry

    lax.fori_loop(0, 16, res_each, 0)

    def chunk1(i, a, d, start, size):
        cols = pl.ds(a * wide, wide)
        if a == 0:
            return pbuf.at[i, d, pl.ds(start, size), :, cols]
        return pbuf.at[i, pl.ds(start, size), d, :, cols]

    def chunk2(i, a, d, start, size):
        cols = pl.ds(a * wide + start, size)
        if a == 0:
            return pbuf.at[i, x, d, :, cols]
        return pbuf.at[i, d, y, :, cols]

    def hop(i, a, s, n):
        sems = rs_send.at[i, a, s, n], rs_recv.at[i, a, s, n]
        near = (1, 3)[n]
        if s == 0:
            return remote(chunk1(i, a, (first[a] + 2) % 4, 2 * n, 2), r1.at[a, i, n], *sems, first_devs[a][n])
        if s == 1:
            return remote(chunk1(i, a, (first[a] + near) % 4, 0, 4), r2.at[a, i, n], *sems, first_devs[a][n])
        if s == 2:
            src = chunk2(i, a, (second[a] + 2) % 4, n * wide // 2, wide // 2)
            return remote(src, r3.at[a, i, n], *sems, second_devs[a][n])
        return remote(chunk2(i, a, (second[a] + near) % 4, 0, wide), r4.at[a, i, n], *sems, second_devs[a][n])

    def pair_hop(i):
        return remote(zs.at[i], zr.at[i], rs_send.at[i, 0, 4, 0], rs_recv.at[i, 0, 4, 0], pair)

    def multiply(i):
        w, h = block(i)

        @pl.when(i == 0)
        def _():
            own_copy.wait()

        @pl.when(i >= 2)
        def _():
            remote(hbuf.at[w, h], hbuf.at[w, h], ag_send.at[0], ag_recv.at[i], mate).wait_recv()

        @pl.when(i == 4)
        def _():
            far_send(i, 0).start()

        @pl.when(i == 9)
        def _():
            far_send(i, 1).start()

        @pl.when(jnp.logical_and(i >= 4, i % 4 < 2))
        def _():
            mate_send(i).start()

        @pl.when(i == 12)
        def _():
            qw_pair.start()

        rows = hbuf[w, h]
        for n in range(0, 2 * wide, 512):
            part = jnp.dot(rows, weight[:, n : n + 512], preferred_element_type=F32)
            pbuf[i, :, :, :, pl.ds(n, 512)] = part.astype(BF16).reshape(4, 4, 16, 512)
        for a in range(2):
            for n in range(2):
                hop(i, a, 0, n).start()

    def relay1(i):
        for a in range(2):
            for n in range(2):
                hop(i, a, 0, n).wait_recv()
                ref = chunk1(i, a, (first[a] + (1, 3)[n]) % 4, 2 * n, 2)
                ref[...] = add(ref[...], r1[a, i, n]).astype(BF16)
                hop(i, a, 1, n).start()

    def turn(i):
        for a in range(2):
            for n in range(2):
                hop(i, a, 1, n).wait_recv()
            ref = chunk1(i, a, first[a], 0, 4)
            ref[...] = add(ref[...], r2[a, i, 0], r2[a, i, 1]).astype(BF16)
            for n in range(2):
                hop(i, a, 2, n).start()

    def relay2(i):
        for a in range(2):
            for n in range(2):
                hop(i, a, 2, n).wait_recv()
                ref = chunk2(i, a, (second[a] + (1, 3)[n]) % 4, n * wide // 2, wide // 2)
                ref[...] = add(ref[...], r3[a, i, n]).astype(BF16)
                hop(i, a, 3, n).start()

    def plane_sum(i):
        for a in range(2):
            for n in range(2):
                hop(i, a, 3, n).wait_recv()
            total = add(chunk2(i, a, second[a], 0, wide)[...], r4[a, i, 0], r4[a, i, 1])

            @pl.when(zlo == a)
            def _():
                acc[i] = total

            @pl.when(zlo != a)
            def _():
                zs[i] = total.astype(BF16)
                pair_hop(i).start()

    def finish(i):
        w, h = block(i)

        @pl.when(i == 0)
        def _():
            pltpu.make_async_copy(rbuf, rbuf, res_recv).wait()

        pair_hop(i).wait_recv()
        sbuf[h, w] = add(acc[i], zr[i], rbuf[h, w]).astype(BF16)

    stages = (multiply, relay1, turn, relay2, plane_sum, finish)

    def body(t, carry):
        for n in (0, 5, 4, 3, 2, 1):
            i = t - n * LAG

            @pl.when(jnp.logical_and(i >= 0, i < UNITS))
            def _():
                stages[n](i)
        return carry

    lax.fori_loop(0, UNITS + 5 * LAG, body, 0)

    tokens = sbuf.shape[1] * sbuf.shape[2]
    lane = lax.broadcasted_iota(jnp.int32, (tokens, tokens), 1)
    row = lax.broadcasted_iota(jnp.int32, (tokens, tokens), 0)
    for q in range(2):
        values = sbuf[q].reshape(tokens, wide).astype(F32)
        mean = jnp.mean(values, axis=1, keepdims=True)
        m2 = jnp.sum((values - mean) ** 2, axis=1, keepdims=True)
        stats[me, q] = jnp.where(lane == 0, mean, m2).T[:8]

    def stat_copy(n):
        dev = (n // 2 % 2, tok, n // 4 * 2 + n % 2)
        return remote(stats.at[me], stats.at[me], st_send.at[n], st_recv.at[me], dev)

    def others(action):
        def step(n, carry):
            pl.when(n != me)(lambda: action(n))
            return carry

        lax.fori_loop(0, 16, step, 0)

    others(lambda n: stat_copy(n).start())

    def out_copy(n, local):
        group = source + n // 8
        src = sbuf.at[:, n % 8, :, pl.ds(pl.multiple_of(n // 8 * narrow, narrow), narrow)]
        dst = stream.at[:, tok]
        if local:
            return pltpu.make_async_copy(src, dst, so_recv)
        return remote(src, dst, so_send.at[n], so_recv, (group // 16, group % 16, n % 8))

    def out_self(n):
        return jnp.logical_and(source + n // 8 == zlo * 16 + tok, n % 8 == wid)

    def out_each(n, carry):
        @pl.when(out_self(n))
        def _():
            out_copy(n, True).start()

        @pl.when(jnp.logical_not(out_self(n)))
        def _():
            out_copy(n, False).start()
        return carry

    lax.fori_loop(0, 16, out_each, 0)

    for n in range(6):
        own_send(n).wait_send()
    for i in (4, 5, 8, 9, 12, 13):
        mate_send(i).wait_send()
    far_send(4, 0).wait_send()
    far_send(9, 1).wait_send()

    def res_done(n, carry):
        @pl.when(jnp.logical_not(jnp.logical_and(res_self, n == tok)))
        def _():
            res_copy(n, False).wait_send()
        return carry

    lax.fori_loop(0, 16, res_done, 0)

    def drain(i, carry):
        for a in range(2):
            for s in range(4):
                for n in range(2):
                    hop(i, a, s, n).wait_send()
        pair_hop(i).wait_send()
        return carry

    lax.fori_loop(0, UNITS, drain, 0)


    def stat_wait(n):
        here = stats.at[n]
        remote(here, here, st_send.at[n], st_recv.at[n], mate).wait_recv()

    others(stat_wait)
    for q in range(2):
        means, m2s = stats[:, q, 0, :], stats[:, q, 1, :]
        mean = jnp.mean(means, axis=0, keepdims=True)
        var = jnp.sum(m2s, axis=0, keepdims=True) + wide * jnp.sum((means - mean) ** 2, axis=0, keepdims=True)
        scale = lax.rsqrt(var / (16 * wide) + norm_eps)
        both = jnp.where(row == 0, mean, scale).T
        values = sbuf[q].reshape(tokens, wide).astype(F32)
        normed = (values - both[:, 0:1]) * both[:, 1:2] * gain[zlo] + shift[zlo]
        nbuf[q, 0] = normed.astype(BF16)

    mid = tokens // 2

    def pass_on(q, u, to, slot, dev, part=None):
        if part is None:
            src, dst = nbuf.at[q, u], nbuf.at[q, to]
        else:
            rows = pl.ds(part * mid, mid)
            src, dst = nbuf.at[q, u, rows], nbuf.at[q, to, rows]
        return remote(src, dst, n_send.at[q, u, slot], n_recv.at[q, to, part or 0], dev)

    def passes(q, u):
        (fp, fm), (sp, sm) = first_devs[q], second_devs[q]
        return (
            (u == 0, lambda: pass_on(q, u, 1, 0, fp)),
            (u == 0, lambda: pass_on(q, u, 2, 1, fm)),
            (u == 1, lambda: pass_on(q, u, 3, 0, fp, 0)),
            (u == 2, lambda: pass_on(q, u, 3, 1, fm, 1)),
            (u < 4, lambda: pass_on(q, u, 4 + u, 2, sp)),
            (u < 4, lambda: pass_on(q, u, 8 + u, 3, sm)),
            (u // 4 == 1, lambda: pass_on(q, u, 8 + u, 2, sp, 0)),
            (u // 4 == 2, lambda: pass_on(q, u, 4 + u, 3, sm, 1)),
        )

    def offset(e):
        return 3 * e + 3 * (e // 2) + 2 * (e // 3)

    def owned(q, u):
        return pbuf.at[u, pl.ds(2 * q, 2), :, :, pl.ds(0, narrow)]

    def given(q, u):
        return pbuf.at[u, pl.ds(2 * q, 2), :, :, pl.ds(narrow, narrow)]

    def mate_copy(q, u):
        return remote(given(q, u), cbuf.at[q, u], c_send.at[q, u], c_recv.at[q, u], mate)

    def multiply2(u):
        for q in range(2):
            split = jnp.logical_or(u == 3, u >= 12)

            @pl.when(jnp.logical_and(u > 0, jnp.logical_not(split)))
            def _():
                here = nbuf.at[q, u]
                remote(here, here, n_send.at[q, u, 0], n_recv.at[q, u, 0], mate).wait_recv()

            @pl.when(split)
            def _():
                for part in range(2):
                    here = nbuf.at[q, u, pl.ds(part * mid, mid)]
                    remote(here, here, n_send.at[q, u, 0], n_recv.at[q, u, part], mate).wait_recv()

            for cond, copy in passes(q, u):
                @pl.when(cond)
                def _():
                    copy().start()

        @pl.when(u == 0)
        def _():
            qw_own.wait()
            qw_pair.wait()
            bias_mate.wait()

        for q in range(2):
            rows = nbuf[q, u]
            part = jnp.dot(rows, qwm[1 - c], preferred_element_type=F32)
            given(q, u)[...] = part.astype(BF16).reshape(2, 4, 16, narrow)
            mate_copy(q, u).start()
            part = jnp.dot(rows, qwm[c], preferred_element_type=F32)
            owned(q, u)[...] = part.astype(BF16).reshape(2, 4, 16, narrow)

    def rel(q):
        return (z + 16 - 2 * (2 * c + x // 2) - q) % 8

    def z_copy(q, u):
        r = rel(q)
        far = r // 4
        at4 = (r == 4).astype(jnp.int32)
        down_way = at4 * (u % 2) + (1 - at4) * far
        to = (z + 8 + 2 * down_way - 1) % 8
        dev = (to % 2, tok, to // 2 * 2 + c)
        return remote(owned(q, u), zbuf.at[down_way, q, u], z_send.at[q, u], z_recv.at[down_way, q, u], dev)

    def z_wait(q, u, side):
        here = zbuf.at[side, q, u]
        remote(here, here, z_send.at[q, u], z_recv.at[side, q, u], mate).wait_recv()

    def fin_copy(q, u, local):
        one, two = offset(u % 4), offset(u // 4)
        to = ((x + one) % 4 * 4 + (y + two) % 4, (x + two) % 4 * 4 + (y + one) % 4)[q]
        dst = query.at[:, :, pl.ds(pl.multiple_of(y * narrow, narrow), narrow)]
        if local:
            return pltpu.make_async_copy(fin.at[u], dst, f_recv.at[y])
        return remote(fin.at[u], dst, f_send.at[u], f_recv.at[y], (zlo, to, zhi * 2 + x % 2))

    def relay(q, u):
        r = rel(q)
        here = owned(q, u)
        mate_copy(q, u).wait_recv()
        side = r // 4
        takes = jnp.logical_or(
            jnp.logical_or(r == 1, r == 2),
            jnp.logical_or(r >= 6, jnp.logical_or(
                jnp.logical_and(r == 3, u % 2 == 0), jnp.logical_and(r == 5, u % 2 == 1)
            )),
        )

        @pl.when(takes)
        def _():
            z_wait(q, u, side)
            here[...] = add(here[...], cbuf[q, u], zbuf[side, q, u]).astype(BF16)

        @pl.when(jnp.logical_and(jnp.logical_not(takes), r != 0))
        def _():
            here[...] = add(here[...], cbuf[q, u]).astype(BF16)

        @pl.when(r != 0)
        def _():
            z_copy(q, u).start()

        @pl.when(r == 0)
        def _():
            z_wait(q, u, 0)
            z_wait(q, u, 1)
            total = add(here[...], cbuf[q, u], zbuf[0, q, u], zbuf[1, q, u]).reshape(8, 16, narrow)
            fin[u] = (total + bias2[x % 2, y][0:1].reshape(1, 1, narrow)).astype(BF16)
            self_too = jnp.logical_and(u == 0, f_self)

            @pl.when(self_too)
            def _():
                fin_copy(q, u, True).start()

            @pl.when(jnp.logical_not(self_too))
            def _():
                fin_copy(q, u, False).start()

    def body2(t, carry):
        @pl.when(t < UNITS)
        def _():
            multiply2(t)

        for q in range(2):
            r = rel(q)
            u = t - LAG2 * (1 + (r - 4) * (2 * (r // 4) - 1))

            @pl.when(jnp.logical_and(u >= 0, u < UNITS))
            def _():
                relay(q, u)
        return carry

    lax.fori_loop(0, UNITS + 5 * LAG2, body2, 0)

    pltpu.make_async_copy(stream, stream, so_recv).wait()
    for n in range(4):
        dst = query.at[:, :, pl.ds(n * narrow, narrow)]
        pltpu.make_async_copy(dst, dst, f_recv.at[n]).wait()
    others(lambda n: stat_copy(n).wait_send())

    def out_done(n, carry):
        @pl.when(jnp.logical_not(out_self(n)))
        def _():
            out_copy(n, False).wait_send()
        return carry

    lax.fori_loop(0, 16, out_done, 0)

    def drain2(u, carry):
        for q in range(2):
            for cond, copy in passes(q, u):
                @pl.when(cond)
                def _():
                    copy().wait_send()
            mate_copy(q, u).wait_send()

            @pl.when(rel(q) != 0)
            def _():
                z_copy(q, u).wait_send()

            @pl.when(jnp.logical_and(rel(q) == 0, jnp.logical_not(jnp.logical_and(u == 0, f_self))))
            def _():
                fin_copy(q, u, False).wait_send()
        return carry

    lax.fori_loop(0, UNITS, drain2, 0)


def per_device(
    hidden, resid, down_weight, down_bias, norm_gain, norm_shift, query_weight, query_bias
):
    rows, depth = hidden.shape
    width = down_weight.shape[1]
    wide = width // 2
    narrow = resid.shape[1]
    dma = pltpu.SemaphoreType.DMA
    vmem = pl.BlockSpec(memory_space=pltpu.VMEM)
    hbm = pl.BlockSpec(memory_space=pl.ANY)
    stream, query = pl.pallas_call(
        layer_kernel,
        out_shape=(
            jax.ShapeDtypeStruct((2, 16, 16, narrow), BF16),
            jax.ShapeDtypeStruct((8, 16, width), BF16),
        ),
        in_specs=[hbm, vmem, vmem, vmem, vmem, vmem, hbm, vmem],
        out_specs=(vmem, vmem),
        scratch_shapes=[
            pltpu.VMEM((8, 2, rows // 2, depth), BF16),
            pltpu.VMEM((2, 16, 16, narrow), BF16),
            pltpu.VMEM((2, 8, 16, wide), BF16),
            pltpu.VMEM((UNITS, 4, 4, 16, width), BF16),
            pltpu.VMEM((2, UNITS, 2, 2, 16, wide), BF16),
            pltpu.VMEM((2, UNITS, 2, 4, 16, wide), BF16),
            pltpu.VMEM((2, UNITS, 2, 16, wide // 2), BF16),
            pltpu.VMEM((2, UNITS, 2, 16, wide), BF16),
            pltpu.VMEM((UNITS, 16, wide), BF16),
            pltpu.VMEM((UNITS, 16, wide), BF16),
            pltpu.VMEM((UNITS, 16, wide), F32),
            pltpu.VMEM((2, 8, 16, wide), BF16),
            pltpu.VMEM((16, 2, 8, 128), F32),
            pltpu.VMEM((2, UNITS, 128, wide), BF16),
            pltpu.VMEM((2, wide, narrow), BF16),
            pltpu.VMEM((2, 4, 8, narrow), F32),
            pltpu.VMEM((2, UNITS, 2, 4, 16, narrow), BF16),
            pltpu.VMEM((2, 2, UNITS, 2, 4, 16, narrow), BF16),
            pltpu.VMEM((UNITS, 8, 16, narrow), BF16),
            dma,
            dma((24,)),
            dma((16,)),
            dma((16,)),
            dma,
            dma((UNITS, 2, 5, 2)),
            dma((UNITS, 2, 5, 2)),
            dma((3,)),
            dma((2,)),
            dma((16,)),
            dma((16,)),
            dma((16,)),
            dma,
            dma((2, UNITS, 4)),
            dma((2, UNITS, 2)),
            dma((2, UNITS)),
            dma((2, UNITS)),
            dma((2, UNITS)),
            dma((2, 2, UNITS)),
            dma((UNITS,)),
            dma((4,)),
        ],
        compiler_params=pltpu.CompilerParams(
            collective_id=0, has_side_effects=True, vmem_limit_bytes=62 * 1024 * 1024
        ),
        cost_estimate=pl.CostEstimate(
            flops=16 * rows * depth * width + 16 * rows * wide * wide,
            bytes_accessed=2 * (rows * depth + depth * width),
            transcendentals=0,
        ),
    )(
        hidden.reshape(2, rows // 2, depth),
        resid.reshape(2, 16, 16, narrow),
        down_bias.reshape(1, narrow),
        down_weight,
        norm_gain.reshape(2, 1, wide),
        norm_shift.reshape(2, 1, wide),
        query_weight.reshape(2, wide, narrow),
        jnp.broadcast_to(query_bias.reshape(4, 1, narrow), (4, 8, narrow)),
    )
    return (stream.reshape(rows, narrow), query)


def solution(mesh):
    return jax.shard_map(
        per_device,
        mesh=mesh,
        in_specs=(
            P("wid", ST),
            P("wid", ST),
            P(ST, "wid"),
            P(ST),
            P("wid"),
            P("wid"),
            P("wid", ST),
            P("wid"),
        ),
        out_specs=(P("wid", ST), P(None, ST, "wid")),
        check_vma=False,
    )
```

```python
import functools

import jax
import jax.numpy as jnp
from jax import lax
from jax.experimental import pallas as pl
from jax.experimental.pallas import tpu as pltpu
from jax.sharding import PartitionSpec as P

norm_eps = 1e-05
ST = ("section", "tok")
F32, BF16 = jnp.float32, jnp.bfloat16
MESH = pl.DeviceIdType.MESH
UNITS = 16
LAG = 2
BEAT = 6
ORDER = (0, 4, 3, 2, 1)
PACE = True
LOOK = 1
WALK = (0, 1, 2, 4, 8, 3, 5, 9, 6, 10, 12, 7, 11, 13, 14, 15)
LAG2 = 2
OUT_AT = 0
EARLY = True


def add(*terms):
    total = terms[0].astype(F32)
    for term in terms[1:]:
        total = total + term.astype(F32)
    return total


def place():
    zlo, tok, wid = (lax.axis_index(name) for name in ("section", "tok", "wid"))
    return zlo, tok // 4, tok % 4, wid // 2, wid % 2


def layer_kernel(
    hidden, resid, bias, weight, gain, shift, qweight, qbias, stream, query,
    hbuf, rsrc, rmid, rbuf, pbuf, r1, r2, r3, r4, zs, zr, acc,
    sbuf, stats, nbuf, qwm, bias2, cbuf, zbuf, fin,
    own_sem, ag_send, ag_recv, res_send, res_recv, rs_send, rs_recv,
    qw_sem, b_sem, st_send, st_recv, so_send, so_recv, n_send, n_recv,
    c_send, c_recv, z_send, z_recv, f_send, f_recv,
):
    zlo, x, y, zhi, c = place()
    tok, wid = x * 4 + y, zhi * 2 + c
    half = hbuf.shape[3]
    wide = weight.shape[1] // 2
    first, second = (x, y), (y, x)
    x_devs = [{"tok": (x + 1) % 4 * 4 + y}, {"tok": (x + 3) % 4 * 4 + y}]
    y_devs = [{"tok": x * 4 + (y + 1) % 4}, {"tok": x * 4 + (y + 3) % 4}]
    first_devs, second_devs = (x_devs, y_devs), (y_devs, x_devs)
    z_devs = [{"wid": (zhi + 1) % 4 * 2 + c}, {"wid": (zhi + 3) % 4 * 2 + c}]
    mate, pair = {"wid": zhi * 2 + 1 - c}, {"section": 1 - zlo}

    def remote(src, dst, send, recv, dev):
        return pltpu.make_async_remote_copy(src, dst, send, recv, device_id=dev, device_id_type=MESH)

    source = 4 * wid + 2 * zlo
    z = zhi * 2 + zlo
    me = z * 2 + c

    f_self = jnp.logical_and(zhi == 2 * c + x // 2, c == x % 2)

    barrier = pltpu.get_barrier_semaphore()

    def greet(dev):
        pl.semaphore_signal(barrier, inc=1, device_id=dev, device_id_type=MESH)

    for dev in (*x_devs, *y_devs):
        greet(dev)

    def greet_line(n, carry):
        pl.when(n != me)(lambda: greet((n // 2 % 2, tok, n // 4 * 2 + n % 2)))
        return carry

    lax.fori_loop(0, 16, greet_line, 0)

    own_copy = pltpu.make_async_copy(hidden, hbuf.at[wid], own_sem)
    own_copy.start()
    qw_own = pltpu.make_async_copy(qweight.at[zlo], qwm.at[zlo], qw_sem.at[0])
    qw_own.start()
    narrow = resid.shape[3]
    rsrc[...] = (resid[...].astype(F32) + bias[...].reshape(1, 1, 1, -1)).astype(BF16)
    for n in range(4):
        bias2[c, n] = jnp.broadcast_to(qbias[n * narrow : (n + 1) * narrow].reshape(1, narrow), (8, narrow))
    pl.semaphore_wait(barrier, 4 + 15)

    def own_send(n):
        h = n % 2
        dev = (mate, *z_devs)[n // 2]
        step = (2 + h, 4 + 4 * h, 5 + 4 * h)[n // 2]
        return remote(hidden.at[h], hbuf.at[wid, h], ag_send.at[n], ag_recv.at[step], dev)

    for n in (2, 4, 0, 1) if PACE else (2, 4, 0, 3, 5, 1):
        own_send(n).start()

    qw_pair = remote(qweight.at[1 - zlo], qwm.at[zlo], qw_sem.at[1], qw_sem.at[2], pair)
    bias_mate = remote(bias2.at[c], bias2.at[c], b_sem.at[0], b_sem.at[1], mate)
    bias_mate.start()

    def block(i):
        g, k = i // 4, i % 4
        mid = (g + 1) // 2 % 2
        off = mid * (3 - 2 * (k % 2)) + 2 * (g // 3)
        h = mid * (g - 1) + (1 - mid) * (k % 2)
        return (zhi + off) % 4 * 2 + (c + k // 2) % 2, h

    def mate_send(i):
        w, h = block(i)
        return remote(hbuf.at[w, h], hbuf.at[w, h], ag_send.at[8 + i], ag_recv.at[i + 2], mate)

    def far_send(i, n):
        w, h = block(i)
        return remote(hbuf.at[w, h], hbuf.at[w, h], ag_send.at[6 + n], ag_recv.at[12 + n], z_devs[n])

    def res_copy(n, local):
        src, dst = rsrc.at[:, n], rmid.at[tok]
        if local:
            return pltpu.make_async_copy(src, dst, res_recv.at[0])
        return remote(src, dst, res_send.at[0], res_recv.at[0], (zlo, n, wid))

    def res_start(n):
        pl.when(n == tok)(lambda: res_copy(n, True).start())
        pl.when(n != tok)(lambda: res_copy(n, False).start())

    def res_line(n, local):
        src, dst = rmid.at[pl.ds(2 * n, 2)], rbuf.at[wid]
        if local:
            return pltpu.make_async_copy(src, dst, res_recv.at[1])
        dev = (n % 2, tok, (zlo * 2 + n // 4) * 2 + n // 2 % 2)
        return remote(src, dst, res_send.at[1], res_recv.at[1], dev)

    def res_turn():
        sent(rmid, res_recv.at[0])
        for n in range(8):
            same = jnp.logical_and(
                n % 2 == zlo, jnp.logical_and(zlo * 2 + n // 4 == zhi, n // 2 % 2 == c)
            )
            pl.when(same)(lambda: res_line(n, True).start())
            pl.when(jnp.logical_not(same))(lambda: res_line(n, False).start())

    def sent(ref, sem):
        pltpu.make_async_copy(ref, ref, sem).wait()

    def chunk1(i, a, d, start, size):
        cols = pl.ds(a * wide, wide)
        if a == 0:
            return pbuf.at[i, d, pl.ds(start, size), :, cols]
        return pbuf.at[i, pl.ds(start, size), d, :, cols]

    def chunk2(i, a, d, start, size):
        cols = pl.ds(a * wide + start, size)
        if a == 0:
            return pbuf.at[i, x, d, :, cols]
        return pbuf.at[i, d, y, :, cols]

    def hop(i, a, s, n):
        sems = rs_send.at[a, s], rs_recv.at[i, a, s, n]
        near = (1, 3)[n]
        if s == 0:
            return remote(chunk1(i, a, (first[a] + 2) % 4, 2 * n, 2), r1.at[a, i, n], *sems, first_devs[a][n])
        if s == 1:
            return remote(chunk1(i, a, (first[a] + near) % 4, 0, 4), r2.at[a, i, n], *sems, first_devs[a][n])
        if s == 2:
            src = chunk2(i, a, (second[a] + 2) % 4, n * wide // 2, wide // 2)
            return remote(src, r3.at[a, i, n], *sems, second_devs[a][n])
        return remote(chunk2(i, a, (second[a] + near) % 4, 0, wide), r4.at[a, i, n], *sems, second_devs[a][n])

    def pair_hop(i):
        return remote(zs.at[i], zr.at[i], rs_send.at[0, 4], rs_recv.at[i, 0, 4, 0], pair)

    def multiply(i):
        w, h = block(i)

        @pl.when(i == 0)
        def _():
            own_copy.wait()

        @pl.when(i >= 2)
        def _():
            remote(hbuf.at[w, h], hbuf.at[w, h], ag_send.at[0], ag_recv.at[i], mate).wait_recv()

        copies = ((8, far_send(4, 0)), (9, far_send(9, 1)))
        if PACE:
            copies = ((4, own_send(3)), (5, own_send(5)), *copies)
        else:
            copies = ((4, far_send(4, 0)), (9, far_send(9, 1)))
        for step, copy in copies:
            pl.when(i == step)(copy.start)

        @pl.when(jnp.logical_and(i >= 4, i % 4 < 2))
        def _():
            mate_send(i).start()

        pl.when(i == 12)(res_turn)
        pl.when(i == 13)(qw_pair.start)

        rows = hbuf[w, h]
        for n in range(0, 2 * wide, 512):
            part = jnp.dot(rows, weight[:, n : n + 512], preferred_element_type=F32)
            pbuf[i, :, :, :, pl.ds(n, 512)] = part.astype(BF16).reshape(4, 4, 16, 512)
        for a in range(2):
            for n in range(2):
                hop(i, a, 0, n).start()

    def relay1(i):
        for a in range(2):
            for n in range(2):
                hop(i, a, 0, n).wait_recv()
                ref = chunk1(i, a, (first[a] + (1, 3)[n]) % 4, 2 * n, 2)
                ref[...] = add(ref[...], r1[a, i, n]).astype(BF16)
                hop(i, a, 1, n).start()

    def turn(i):
        for a in range(2):
            for n in range(2):
                hop(i, a, 1, n).wait_recv()
            ref = chunk1(i, a, first[a], 0, 4)
            ref[...] = add(ref[...], r2[a, i, 0], r2[a, i, 1]).astype(BF16)
            for n in range(2):
                hop(i, a, 2, n).start()

    def relay2(i):
        for a in range(2):
            for n in range(2):
                hop(i, a, 2, n).wait_recv()
                ref = chunk2(i, a, (second[a] + (1, 3)[n]) % 4, n * wide // 2, wide // 2)
                ref[...] = add(ref[...], r3[a, i, n]).astype(BF16)
                hop(i, a, 3, n).start()

    def plane_sum(i):
        for a in range(2):
            for n in range(2):
                hop(i, a, 3, n).wait_recv()
            total = add(chunk2(i, a, second[a], 0, wide)[...], r4[a, i, 0], r4[a, i, 1])

            @pl.when(zlo == a)
            def _():
                w, h = block(i)
                acc[h, w] = total

            @pl.when(zlo != a)
            def _():
                zs[i] = total.astype(BF16)
                pair_hop(i).start()

    def finish(i):
        w, h = block(i)
        pair_hop(i).wait_recv()
        acc[h, w] = add(acc[h, w], zr[i])

    stages = (multiply, relay1, turn, relay2, plane_sum)

    def body(t, carry):
        for n in ORDER:
            turn_at = t - n * LAG
            i = turn_at // BEAT * 4 + turn_at % BEAT
            due = jnp.logical_and(turn_at % BEAT < 4, i < UNITS)

            @pl.when(jnp.logical_and(turn_at >= 0, due))
            def _():
                stages[n](i)

        @pl.when(jnp.logical_and(t > 4 * LAG, t < 4 * LAG + 5))
        def _():
            for n in range(4):
                res_start(4 * (t - 4 * LAG - 1) + n)
        return carry

    lax.fori_loop(0, 3 * BEAT + 4 + 4 * LAG, body, 0)

    def finish_each(i, carry):
        finish(i)
        return carry

    lax.fori_loop(0, UNITS, finish_each, 0)

    sent(rbuf, res_recv.at[1])
    for q in range(2):
        for n in range(2):
            cols = pl.ds(n * narrow, narrow)
            sbuf[q, :, :, cols] = add(acc[q, :, :, cols], rbuf[:, n, q]).astype(BF16)

    tokens = sbuf.shape[1] * sbuf.shape[2]
    lane = lax.broadcasted_iota(jnp.int32, (tokens, tokens), 1)
    row = lax.broadcasted_iota(jnp.int32, (tokens, tokens), 0)
    for q in range(2):
        values = sbuf[q].reshape(tokens, wide).astype(F32)
        mean = jnp.mean(values, axis=1, keepdims=True)
        m2 = jnp.sum((values - mean) ** 2, axis=1, keepdims=True)
        stats[me, q] = jnp.where(lane == 0, mean, m2).T[:8]

    def stat_copy(n):
        dev = (n // 2 % 2, tok, n // 4 * 2 + n % 2)
        return remote(stats.at[me], stats.at[me], st_send, st_recv.at[me], dev)

    def others(action):
        def step(n, carry):
            pl.when(n != me)(lambda: action(n))
            return carry

        lax.fori_loop(0, 16, step, 0)

    others(lambda n: stat_copy(n).start())

    def out_copy(n, local):
        group = source + n // 8
        src = sbuf.at[:, n % 8, :, pl.ds(pl.multiple_of(n // 8 * narrow, narrow), narrow)]
        dst = stream.at[:, tok]
        if local:
            return pltpu.make_async_copy(src, dst, so_recv)
        return remote(src, dst, so_send, so_recv, (group // 16, group % 16, n % 8))

    def out_self(n):
        return jnp.logical_and(source + n // 8 == zlo * 16 + tok, n % 8 == wid)

    def out_start(n):
        pl.when(out_self(n))(lambda: out_copy(n, True).start())
        pl.when(jnp.logical_not(out_self(n)))(lambda: out_copy(n, False).start())

    for n in range(6):
        own_send(n).wait_send()
    for i in (4, 5, 8, 9, 12, 13):
        mate_send(i).wait_send()
    far_send(4, 0).wait_send()
    far_send(9, 1).wait_send()

    for a in range(2):
        for n, ref in enumerate((r1, r2, r3, r4)):
            sent(ref.at[a], rs_send.at[a, n])
    sent(zr, rs_send.at[0, 4])

    def stat_wait(n):
        here = stats.at[n]
        remote(here, here, st_send, st_recv.at[n], mate).wait_recv()

    others(stat_wait)
    gains, shifts = (
        jnp.where(zlo == 0, ref[0:wide], ref[wide : 2 * wide]).reshape(1, wide) for ref in (gain, shift)
    )
    for q in range(2):
        means, m2s = stats[:, q, 0, :], stats[:, q, 1, :]
        mean = jnp.mean(means, axis=0, keepdims=True)
        var = jnp.sum(m2s, axis=0, keepdims=True) + wide * jnp.sum((means - mean) ** 2, axis=0, keepdims=True)
        scale = lax.rsqrt(var / (16 * wide) + norm_eps)
        both = jnp.where(row == 0, mean, scale).T
        values = sbuf[q].reshape(tokens, wide).astype(F32)
        normed = (values - both[:, 0:1]) * both[:, 1:2] * gains + shifts
        nbuf[q, 0] = normed.astype(BF16)

    mid = tokens // 2

    def pass_on(q, u, to, dev, part=None):
        if part is None:
            src, dst = nbuf.at[q, u], nbuf.at[q, to]
        else:
            rows = pl.ds(part * mid, mid)
            src, dst = nbuf.at[q, u, rows], nbuf.at[q, to, rows]
        return remote(src, dst, n_send.at[q], n_recv.at[q, to, part or 0], dev)

    def passes(q, u):
        (fp, fm), (sp, sm) = first_devs[q], second_devs[q]
        return (
            (u == 0, lambda: pass_on(q, u, 1, fp)),
            (u == 0, lambda: pass_on(q, u, 2, fm)),
            (u == 1, lambda: pass_on(q, u, 3, fp, 0)),
            (u == 2, lambda: pass_on(q, u, 3, fm, 1)),
            (u < 4, lambda: pass_on(q, u, 4 + u, sp)),
            (u < 4, lambda: pass_on(q, u, 8 + u, sm)),
            (u // 4 == 1, lambda: pass_on(q, u, 8 + u, sp, 0)),
            (u // 4 == 2, lambda: pass_on(q, u, 4 + u, sm, 1)),
        )

    def offset(e):
        return 3 * e + 3 * (e // 2) + 2 * (e // 3)

    def owned(q, u):
        return pbuf.at[u, pl.ds(2 * q, 2), :, :, pl.ds(0, narrow)]

    def given(q, u):
        return pbuf.at[u, pl.ds(2 * q, 2), :, :, pl.ds(narrow, narrow)]

    def mate_copy(q, u):
        return remote(given(q, u), cbuf.at[q, u], c_send.at[q], c_recv.at[q, u], mate)

    def walk(k):
        return sum((k == n).astype(jnp.int32) * u for n, u in enumerate(WALK))

    def arrive(u):
        for q in range(2):
            split = jnp.logical_or(u == 3, u >= 12)

            @pl.when(jnp.logical_and(u > 0, jnp.logical_not(split)))
            def _():
                here = nbuf.at[q, u]
                remote(here, here, n_send.at[q], n_recv.at[q, u, 0], mate).wait_recv()

            @pl.when(split)
            def _():
                for part in range(2):
                    here = nbuf.at[q, u, pl.ds(part * mid, mid)]
                    remote(here, here, n_send.at[q], n_recv.at[q, u, part], mate).wait_recv()

            for cond, copy in passes(q, u):
                @pl.when(cond)
                def _():
                    copy().start()

    def multiply2(t):
        @pl.when(t == 0)
        def _():
            arrive(0 * t)
            for n in range(1, LOOK):
                arrive(walk(n + 0 * t))

        pl.when(t < UNITS - LOOK)(lambda: arrive(walk(t + LOOK)))
        u = walk(t)

        @pl.when(t == 0)
        def _():
            qw_own.wait()
            qw_pair.wait()
            bias_mate.wait()

        for q in range(2):
            rows = nbuf[q, u]
            part = jnp.dot(rows, qwm[1 - c], preferred_element_type=F32)
            given(q, u)[...] = part.astype(BF16).reshape(2, 4, 16, narrow)
            mate_copy(q, u).start()
            part = jnp.dot(rows, qwm[c], preferred_element_type=F32)
            owned(q, u)[...] = part.astype(BF16).reshape(2, 4, 16, narrow)

    def rel(q):
        return (z + 16 - 2 * (2 * c + x // 2) - q) % 8

    def z_copy(q, u):
        r = rel(q)
        far = r // 4
        at4 = (r == 4).astype(jnp.int32)
        down_way = at4 * (u % 2) + (1 - at4) * far
        to = (z + 8 + 2 * down_way - 1) % 8
        dev = (to % 2, tok, to // 2 * 2 + c)
        return remote(owned(q, u), zbuf.at[down_way, q, u], z_send.at[q], z_recv.at[down_way, q, u], dev)

    def z_wait(q, u, side):
        here = zbuf.at[side, q, u]
        remote(here, here, z_send.at[q], z_recv.at[side, q, u], mate).wait_recv()

    def fin_copy(q, u, local):
        one, two = offset(u % 4), offset(u // 4)
        to = ((x + one) % 4 * 4 + (y + two) % 4, (x + two) % 4 * 4 + (y + one) % 4)[q]
        dst = query.at[:, :, pl.ds(pl.multiple_of(y * narrow, narrow), narrow)]
        if local:
            return pltpu.make_async_copy(fin.at[u], dst, f_recv.at[y])
        return remote(fin.at[u], dst, f_send, f_recv.at[y], (zlo, to, zhi * 2 + x % 2))

    def relay(q, u):
        r = rel(q)
        here = owned(q, u)
        mate_copy(q, u).wait_recv()
        side = r // 4
        takes = jnp.logical_or(
            jnp.logical_or(r == 1, r == 2),
            jnp.logical_or(r >= 6, jnp.logical_or(
                jnp.logical_and(r == 3, u % 2 == 0), jnp.logical_and(r == 5, u % 2 == 1)
            )),
        )

        @pl.when(takes)
        def _():
            z_wait(q, u, side)
            here[...] = add(here[...], cbuf[q, u], zbuf[side, q, u]).astype(BF16)

        @pl.when(jnp.logical_and(jnp.logical_not(takes), r != 0))
        def _():
            here[...] = add(here[...], cbuf[q, u]).astype(BF16)

        @pl.when(r != 0)
        def _():
            z_copy(q, u).start()

        @pl.when(r == 0)
        def _():
            z_wait(q, u, 0)
            z_wait(q, u, 1)
            total = add(here[...], cbuf[q, u], zbuf[0, q, u], zbuf[1, q, u]).reshape(8, 16, narrow)
            fin[u] = (total + bias2[x % 2, y][0:1].reshape(1, 1, narrow)).astype(BF16)
            self_too = jnp.logical_and(u == 0, f_self)

            @pl.when(self_too)
            def _():
                fin_copy(q, u, True).start()

            @pl.when(jnp.logical_not(self_too))
            def _():
                fin_copy(q, u, False).start()

    def body2(t, carry):
        if EARLY:
            pl.when(t < UNITS)(lambda: multiply2(t))
        for q in range(2):
            r = rel(q)
            k = t - LAG2 * (1 + (r - 4) * (2 * (r // 4) - 1))

            @pl.when(jnp.logical_and(k >= 0, k < UNITS))
            def _():
                relay(q, walk(k))

        if not EARLY:
            pl.when(t < UNITS)(lambda: multiply2(t))

        @pl.when(jnp.logical_and(t >= OUT_AT, t < OUT_AT + 8))
        def _():
            for n in range(2):
                out_start(2 * (t - OUT_AT) + n)
        return carry

    lax.fori_loop(0, UNITS + 5 * LAG2, body2, 0)

    pltpu.make_async_copy(stream, stream, so_recv).wait()
    for n in range(4):
        dst = query.at[:, :, pl.ds(n * narrow, narrow)]
        pltpu.make_async_copy(dst, dst, f_recv.at[n]).wait()
    sent(stats.at[pl.ds(0, 15)], st_send)
    for q in range(2):
        sent(nbuf.at[q, pl.ds(0, 15)], n_send.at[q])
        sent(cbuf.at[q], c_send.at[q])
        pl.when(rel(q) != 0)(lambda: sent(zbuf.at[0, q], z_send.at[q]))
    sent(rsrc.at[:, pl.ds(0, 15)], res_send.at[0])
    res_self = zhi // 2 == zlo
    pl.when(res_self)(lambda: sent(rbuf.at[pl.ds(0, 7)], res_send.at[1]))
    pl.when(jnp.logical_not(res_self))(lambda: sent(rbuf, res_send.at[1]))
    out_own = jnp.logical_and(zhi == 2 * zlo + x // 2, jnp.logical_and(c == x % 2, zlo == y // 2))
    pl.when(out_own)(lambda: sent(rsrc.at[:, pl.ds(0, 15)], so_send))
    pl.when(jnp.logical_not(out_own))(lambda: sent(rsrc, so_send))
    f_dest = zhi == 2 * c + x // 2
    pl.when(f_self)(lambda: sent(fin.at[pl.ds(0, 15)], f_send))
    pl.when(jnp.logical_and(f_dest, jnp.logical_not(f_self)))(lambda: sent(fin, f_send))


def per_device(
    hidden, resid, down_weight, down_bias, norm_gain, norm_shift, query_weight, query_bias
):
    rows, depth = hidden.shape
    width = down_weight.shape[1]
    wide = width // 2
    narrow = resid.shape[1]
    dma = pltpu.SemaphoreType.DMA
    vmem = pl.BlockSpec(memory_space=pltpu.VMEM)
    hbm = pl.BlockSpec(memory_space=pl.ANY)
    stream, query = pl.pallas_call(
        layer_kernel,
        out_shape=(
            jax.ShapeDtypeStruct((2, 16, 16, narrow), BF16),
            jax.ShapeDtypeStruct((8, 16, width), BF16),
        ),
        in_specs=[hbm, vmem, vmem, vmem, vmem, vmem, hbm, vmem],
        out_specs=(vmem, vmem),
        scratch_shapes=[
            pltpu.VMEM((8, 2, rows // 2, depth), BF16),
            pltpu.VMEM((2, 16, 16, narrow), BF16),
            pltpu.VMEM((16, 2, 16, narrow), BF16),
            pltpu.VMEM((8, 2, 2, 16, narrow), BF16),
            pltpu.VMEM((UNITS, 4, 4, 16, width), BF16),
            pltpu.VMEM((2, UNITS, 2, 2, 16, wide), BF16),
            pltpu.VMEM((2, UNITS, 2, 4, 16, wide), BF16),
            pltpu.VMEM((2, UNITS, 2, 16, wide // 2), BF16),
            pltpu.VMEM((2, UNITS, 2, 16, wide), BF16),
            pltpu.VMEM((UNITS, 16, wide), BF16),
            pltpu.VMEM((UNITS, 16, wide), BF16),
            pltpu.VMEM((2, 8, 16, wide), F32),
            pltpu.VMEM((2, 8, 16, wide), BF16),
            pltpu.VMEM((16, 2, 8, 128), F32),
            pltpu.VMEM((2, UNITS, 128, wide), BF16),
            pltpu.VMEM((2, wide, narrow), BF16),
            pltpu.VMEM((2, 4, 8, narrow), F32),
            pltpu.VMEM((2, UNITS, 2, 4, 16, narrow), BF16),
            pltpu.VMEM((2, 2, UNITS, 2, 4, 16, narrow), BF16),
            pltpu.VMEM((UNITS, 8, 16, narrow), BF16),
            dma,
            dma((24,)),
            dma((16,)),
            dma((2,)),
            dma((2,)),
            dma((2, 5)),
            dma((UNITS, 2, 5, 2)),
            dma((3,)),
            dma((2,)),
            dma,
            dma((16,)),
            dma,
            dma,
            dma((2,)),
            dma((2, UNITS, 2)),
            dma((2,)),
            dma((2, UNITS)),
            dma((2,)),
            dma((2, 2, UNITS)),
            dma,
            dma((4,)),
        ],
        compiler_params=pltpu.CompilerParams(
            collective_id=0, has_side_effects=True, vmem_limit_bytes=62 * 1024 * 1024
        ),
        cost_estimate=pl.CostEstimate(
            flops=16 * rows * depth * width + 16 * rows * wide * wide,
            bytes_accessed=2 * (rows * depth + depth * width),
            transcendentals=0,
        ),
    )(
        hidden.reshape(2, rows // 2, depth),
        resid.reshape(2, 16, 16, narrow),
        down_bias,
        down_weight,
        norm_gain,
        norm_shift,
        query_weight.reshape(2, wide, narrow),
        query_bias,
    )
    return (stream.reshape(rows, narrow), query)


def solution(mesh):
    return jax.shard_map(
        per_device,
        mesh=mesh,
        in_specs=(
            P("wid", ST),
            P("wid", ST),
            P(ST, "wid"),
            P(ST),
            P("wid"),
            P("wid"),
            P("wid", ST),
            P("wid"),
        ),
        out_specs=(P("wid", ST), P(None, ST, "wid")),
        check_vma=False,
    )
```

```python
import functools

import jax
import jax.numpy as jnp
from jax import lax
from jax.experimental import pallas as pl
from jax.experimental.pallas import tpu as pltpu
from jax.sharding import PartitionSpec as P

norm_eps = 1e-05
ST = ("section", "tok")
F32, BF16 = jnp.float32, jnp.bfloat16
MESH = pl.DeviceIdType.MESH
UNITS = 16
LAG = 2
BEAT = 6
ORDER = (4, 3, 2, 1, 0)
LOOK = 1
WALK = (0, 1, 2, 4, 8, 5, 9, 6, 10, 3, 12, 7, 11, 13, 14, 15)
LAG1 = 1
LAG2 = 2
OUT_AT = -1
EARLY = False


def add(*terms):
    total = terms[0].astype(F32)
    for term in terms[1:]:
        total = total + term.astype(F32)
    return total


def place():
    zlo, tok, wid = (lax.axis_index(name) for name in ("section", "tok", "wid"))
    return zlo, tok // 4, tok % 4, wid // 2, wid % 2


def layer_kernel(
    hidden, resid, bias, weight, gain, shift, qweight, qbias, stream, query,
    hbuf, rsrc, rmid, rbuf, pbuf, r1, r2, r3, r4, zs, zr, acc,
    sbuf, stats, nbuf, qwm, bias2, cbuf, zbuf, fin,
    own_sem, ag_send, ag_recv, res_send, res_recv, rs_send, rs_recv,
    qw_sem, b_sem, st_send, st_recv, so_send, so_recv, n_send, n_recv,
    c_send, c_recv, z_send, z_recv, f_send, f_recv,
):
    zlo, x, y, zhi, c = place()
    tok, wid = x * 4 + y, zhi * 2 + c
    half = hbuf.shape[3]
    wide = weight.shape[1] // 2
    first, second = (x, y), (y, x)
    x_devs = [{"tok": (x + 1) % 4 * 4 + y}, {"tok": (x + 3) % 4 * 4 + y}]
    y_devs = [{"tok": x * 4 + (y + 1) % 4}, {"tok": x * 4 + (y + 3) % 4}]
    first_devs, second_devs = (x_devs, y_devs), (y_devs, x_devs)
    z_devs = [{"wid": (zhi + 1) % 4 * 2 + c}, {"wid": (zhi + 3) % 4 * 2 + c}]
    mate, pair = {"wid": zhi * 2 + 1 - c}, {"section": 1 - zlo}

    def remote(src, dst, send, recv, dev):
        return pltpu.make_async_remote_copy(src, dst, send, recv, device_id=dev, device_id_type=MESH)

    source = 4 * wid + 2 * zlo
    z = zhi * 2 + zlo
    me = z * 2 + c

    f_self = jnp.logical_and(zhi == 2 * c + x // 2, c == x % 2)

    barrier = pltpu.get_barrier_semaphore()

    def greet(dev):
        pl.semaphore_signal(barrier, inc=1, device_id=dev, device_id_type=MESH)

    for dev in (*x_devs, *y_devs):
        greet(dev)

    for dev in (*z_devs, mate, pair, {"section": 1 - zlo, "wid": (zhi + 3 + 2 * zlo) % 4 * 2 + c}):
        greet(dev)

    own_copy = pltpu.make_async_copy(hidden, hbuf.at[wid], own_sem)
    own_copy.start()
    narrow = resid.shape[3]
    place_at = pl.ds(pl.multiple_of((zlo + c) % 2 * narrow, narrow), narrow)
    qw_own = pltpu.make_async_copy(qweight.at[zlo], qwm.at[:, place_at], qw_sem.at[0])
    qw_own.start()
    rsrc[...] = (resid[...].astype(F32) + bias[...].reshape(1, 1, 1, -1)).astype(BF16)
    for n in range(4):
        bias2[c, n] = jnp.broadcast_to(qbias[n * narrow : (n + 1) * narrow].reshape(1, narrow), (8, narrow))
    pl.semaphore_wait(barrier, 4 + 5)

    def own_send(n):
        h = n % 2
        dev = (mate, *z_devs)[n // 2]
        step = (2 + h, 4 + 4 * h, 9 - 4 * h)[n // 2]
        return remote(hidden.at[h], hbuf.at[wid, h], ag_send.at[n], ag_recv.at[step], dev)

    for n in (2, 5, 0, 1):
        own_send(n).start()

    qw_pair = remote(qweight.at[1 - zlo], qwm.at[:, place_at], qw_sem.at[1], qw_sem.at[2], pair)
    bias_mate = remote(bias2.at[c], bias2.at[c], b_sem.at[0], b_sem.at[1], mate)
    bias_mate.start()

    def block(i):
        g, k = i // 4, i % 4
        mid = (g + 1) // 2 % 2
        off = mid * (3 - 2 * (k % 2)) + 2 * (g // 3)
        h = (k + mid * (g - 1)) % 2
        return (zhi + off) % 4 * 2 + (c + k // 2) % 2, h

    def mate_send(i):
        w, h = block(i)
        return remote(hbuf.at[w, h], hbuf.at[w, h], ag_send.at[8 + i], ag_recv.at[i + 2], mate)

    def far_send(i, n):
        w, h = block(i)
        return remote(hbuf.at[w, h], hbuf.at[w, h], ag_send.at[6 + n], ag_recv.at[12 + n], z_devs[n])

    def res_copy(n, local):
        src, dst = rsrc.at[:, n], rmid.at[tok]
        if local:
            return pltpu.make_async_copy(src, dst, res_recv.at[0])
        return remote(src, dst, res_send.at[0], res_recv.at[0], (zlo, n, wid))

    def res_start(n):
        pl.when(n == tok)(lambda: res_copy(n, True).start())
        pl.when(n != tok)(lambda: res_copy(n, False).start())

    def res_line(n, local):
        src, dst = rmid.at[pl.ds(2 * n, 2)], rbuf.at[wid]
        if local:
            return pltpu.make_async_copy(src, dst, res_recv.at[1])
        dev = (n % 2, tok, (zlo * 2 + n // 4) * 2 + n // 2 % 2)
        return remote(src, dst, res_send.at[1], res_recv.at[1], dev)

    def res_turn():
        sent(rmid, res_recv.at[0])
        for n in range(8):
            same = jnp.logical_and(
                n % 2 == zlo, jnp.logical_and(zlo * 2 + n // 4 == zhi, n // 2 % 2 == c)
            )
            pl.when(same)(lambda: res_line(n, True).start())
            pl.when(jnp.logical_not(same))(lambda: res_line(n, False).start())

    def sent(ref, sem):
        pltpu.make_async_copy(ref, ref, sem).wait()

    def chunk1(i, a, d, start, size):
        cols = pl.ds(a * wide, wide)
        if a == 0:
            return pbuf.at[i, d, pl.ds(start, size), :, cols]
        return pbuf.at[i, pl.ds(start, size), d, :, cols]

    def chunk2(i, a, d, start, size):
        cols = pl.ds(a * wide + start, size)
        if a == 0:
            return pbuf.at[i, x, d, :, cols]
        return pbuf.at[i, d, y, :, cols]

    def hop(i, a, s, n):
        sems = rs_send.at[a, s], rs_recv.at[i, a, s, n]
        near = (1, 3)[n]
        if s == 0:
            return remote(chunk1(i, a, (first[a] + 2) % 4, 2 * n, 2), r1.at[a, i, n], *sems, first_devs[a][n])
        if s == 1:
            return remote(chunk1(i, a, (first[a] + near) % 4, 0, 4), r2.at[a, i, n], *sems, first_devs[a][n])
        if s == 2:
            src = chunk2(i, a, (second[a] + 2) % 4, n * wide // 2, wide // 2)
            return remote(src, r3.at[a, i, n], *sems, second_devs[a][n])
        return remote(chunk2(i, a, (second[a] + near) % 4, 0, wide), r4.at[a, i, n], *sems, second_devs[a][n])

    def pair_hop(i):
        return remote(zs.at[i], zr.at[i], rs_send.at[0, 4], rs_recv.at[i, 0, 4, 0], pair)

    def multiply(i):
        w, h = block(i)

        @pl.when(i == 0)
        def _():
            own_copy.wait()

        for step, gone, then in ((4, (2, 5), (own_send(3), own_send(4))), (8, (3, 4), (far_send(4, 0), far_send(5, 1)))):
            @pl.when(i == step)
            def _():
                for n, copy in zip(gone, then):
                    own_send(n).wait_send()
                    copy.start()

        @pl.when(i >= 2)
        def _():
            remote(hbuf.at[w, h], hbuf.at[w, h], ag_send.at[0], ag_recv.at[i], mate).wait_recv()

        @pl.when(jnp.logical_and(i >= 4, i % 4 < 2))
        def _():
            mate_send(i).start()

        pl.when(i == 12)(res_turn)
        pl.when(i == 13)(qw_pair.start)

        rows = hbuf[w, h]
        for n in range(0, 2 * wide, 512):
            part = jnp.dot(rows, weight[:, n : n + 512], preferred_element_type=F32)
            pbuf[i, :, :, :, pl.ds(n, 512)] = part.astype(BF16).reshape(4, 4, 16, 512)
        for a in range(2):
            for n in range(2):
                hop(i, a, 0, n).start()

    def relay1(i):
        for a in range(2):
            for n in range(2):
                hop(i, a, 0, n).wait_recv()
                ref = chunk1(i, a, (first[a] + (1, 3)[n]) % 4, 2 * n, 2)
                ref[...] = add(ref[...], r1[a, i, n]).astype(BF16)
                hop(i, a, 1, n).start()

    def turn(i):
        for a in range(2):
            for n in range(2):
                hop(i, a, 1, n).wait_recv()
            ref = chunk1(i, a, first[a], 0, 4)
            ref[...] = add(ref[...], r2[a, i, 0], r2[a, i, 1]).astype(BF16)
            for n in range(2):
                hop(i, a, 2, n).start()

    def relay2(i):
        for a in range(2):
            for n in range(2):
                hop(i, a, 2, n).wait_recv()
                ref = chunk2(i, a, (second[a] + (1, 3)[n]) % 4, n * wide // 2, wide // 2)
                ref[...] = add(ref[...], r3[a, i, n]).astype(BF16)
                hop(i, a, 3, n).start()

    def plane_sum(i):
        for a in range(2):
            for n in range(2):
                hop(i, a, 3, n).wait_recv()
            total = add(chunk2(i, a, second[a], 0, wide)[...], r4[a, i, 0], r4[a, i, 1])

            @pl.when(zlo == a)
            def _():
                w, h = block(i)
                acc[h, w] = total

            @pl.when(zlo != a)
            def _():
                zs[i] = total.astype(BF16)
                pair_hop(i).start()

    def finish(i):
        w, h = block(i)
        pair_hop(i).wait_recv()
        acc[h, w] = add(acc[h, w], zr[i])

    stages = (multiply, relay1, turn, relay2, plane_sum)

    def body(t, carry):
        for n in ORDER:
            turn_at = t - n * LAG
            i = turn_at // BEAT * 4 + turn_at % BEAT
            due = jnp.logical_and(turn_at % BEAT < 4, i < UNITS)

            @pl.when(jnp.logical_and(turn_at >= 0, due))
            def _():
                stages[n](i)

        @pl.when(jnp.logical_and(t > 4 * LAG, t < 4 * LAG + 5))
        def _():
            for n in range(4):
                res_start(4 * (t - 4 * LAG - 1) + n)
        return carry

    lax.fori_loop(0, 3 * BEAT + 4 + 4 * LAG, body, 0)

    def finish_each(i, carry):
        finish(i)
        return carry

    lax.fori_loop(0, UNITS, finish_each, 0)

    sent(rbuf, res_recv.at[1])
    for q in range(2):
        for n in range(2):
            cols = pl.ds(n * narrow, narrow)
            sbuf[q, :, :, cols] = add(acc[q, :, :, cols], rbuf[:, n, q]).astype(BF16)

    tokens = sbuf.shape[1] * sbuf.shape[2]
    lane = lax.broadcasted_iota(jnp.int32, (tokens, tokens), 1)
    row = lax.broadcasted_iota(jnp.int32, (tokens, tokens), 0)
    for q in range(2):
        values = sbuf[q].reshape(tokens, wide).astype(F32)
        mean = jnp.mean(values, axis=1, keepdims=True)
        m2 = jnp.sum((values - mean) ** 2, axis=1, keepdims=True)
        stats[me, q] = jnp.where(lane == 0, mean, m2).T[:8]

    def stat_copy(n):
        dev = (n // 2 % 2, tok, n // 4 * 2 + n % 2)
        return remote(stats.at[me], stats.at[me], st_send, st_recv.at[me], dev)

    def others(action):
        def step(n, carry):
            pl.when(n != me)(lambda: action(n))
            return carry

        lax.fori_loop(0, 16, step, 0)

    others(lambda n: stat_copy(n).start())

    def out_copy(n, local):
        group = source + n // 8
        src = sbuf.at[:, n % 8, :, pl.ds(pl.multiple_of(n // 8 * narrow, narrow), narrow)]
        dst = stream.at[:, tok]
        if local:
            return pltpu.make_async_copy(src, dst, so_recv)
        return remote(src, dst, so_send, so_recv, (group // 16, group % 16, n % 8))

    def out_self(n):
        return jnp.logical_and(source + n // 8 == zlo * 16 + tok, n % 8 == wid)

    def out_start(n):
        pl.when(out_self(n))(lambda: out_copy(n, True).start())
        pl.when(jnp.logical_not(out_self(n)))(lambda: out_copy(n, False).start())

    for n in range(2):
        own_send(n).wait_send()
    for i in (4, 5, 8, 9, 12, 13):
        mate_send(i).wait_send()
    far_send(4, 0).wait_send()
    far_send(5, 1).wait_send()

    for a in range(2):
        for n, ref in enumerate((r1, r2, r3, r4)):
            sent(ref.at[a], rs_send.at[a, n])
    sent(zr, rs_send.at[0, 4])

    if OUT_AT < 0:
        def out_each(n, carry):
            out_start(n)
            return carry

        lax.fori_loop(0, 16, out_each, 0)

    def stat_wait(n):
        here = stats.at[n]
        remote(here, here, st_send, st_recv.at[n], mate).wait_recv()

    others(stat_wait)
    gains, shifts = (
        jnp.where(zlo == 0, ref[0:wide], ref[wide : 2 * wide]).reshape(1, wide) for ref in (gain, shift)
    )
    for q in range(2):
        means, m2s = stats[:, q, 0, :], stats[:, q, 1, :]
        mean = jnp.mean(means, axis=0, keepdims=True)
        var = jnp.sum(m2s, axis=0, keepdims=True) + wide * jnp.sum((means - mean) ** 2, axis=0, keepdims=True)
        scale = lax.rsqrt(var / (16 * wide) + norm_eps)
        both = jnp.where(row == 0, mean, scale).T
        values = sbuf[q].reshape(tokens, wide).astype(F32)
        normed = (values - both[:, 0:1]) * both[:, 1:2] * gains + shifts
        nbuf[0, q] = normed.astype(BF16)

    mid = tokens // 2

    def pass_on(q, u, to, dev, part=None):
        if part is None:
            src, dst = nbuf.at[u, q], nbuf.at[to, q]
        else:
            rows = pl.ds(part * mid, mid)
            src, dst = nbuf.at[u, q, rows], nbuf.at[to, q, rows]
        return remote(src, dst, n_send.at[q], n_recv.at[q, to, part or 0], dev)

    def passes(q, u):
        (fp, fm), (sp, sm) = first_devs[q], second_devs[q]
        return (
            (u == 0, lambda: pass_on(q, u, 1, fp)),
            (u == 0, lambda: pass_on(q, u, 2, fm)),
            (u == 1, lambda: pass_on(q, u, 3, fp, 0)),
            (u == 2, lambda: pass_on(q, u, 3, fm, 1)),
            (u < 4, lambda: pass_on(q, u, 4 + u, sp)),
            (u < 4, lambda: pass_on(q, u, 8 + u, sm)),
            (u // 4 == 1, lambda: pass_on(q, u, 8 + u, sp, 0)),
            (u // 4 == 2, lambda: pass_on(q, u, 4 + u, sm, 1)),
        )

    def offset(e):
        return 3 * e + 3 * (e // 2) + 2 * (e // 3)

    def owned(q, u):
        return pbuf.at[u, pl.ds(2 * q, 2), :, :, pl.ds(0, narrow)]

    def given(q, u):
        return pbuf.at[u, pl.ds(2 * q, 2), :, :, pl.ds(narrow, narrow)]

    def mate_copy(q, u):
        return remote(given(q, u), cbuf.at[q, u], c_send.at[q], c_recv.at[q, u], mate)

    def walk(k):
        return sum((k == n).astype(jnp.int32) * u for n, u in enumerate(WALK))

    def arrive(u):
        for q in range(2):
            split = jnp.logical_or(u == 3, u >= 12)

            @pl.when(jnp.logical_and(u > 0, jnp.logical_not(split)))
            def _():
                here = nbuf.at[u, q]
                remote(here, here, n_send.at[q], n_recv.at[q, u, 0], mate).wait_recv()

            @pl.when(split)
            def _():
                for part in range(2):
                    here = nbuf.at[u, q, pl.ds(part * mid, mid)]
                    remote(here, here, n_send.at[q], n_recv.at[q, u, part], mate).wait_recv()

            for cond, copy in passes(q, u):
                @pl.when(cond)
                def _():
                    copy().start()

    def multiply2(t):
        @pl.when(t == 0)
        def _():
            arrive(0 * t)
            for n in range(1, LOOK):
                arrive(walk(n + 0 * t))

        u = walk(t)

        @pl.when(t == 0)
        def _():
            qw_own.wait()
            qw_pair.wait()
            bias_mate.wait()

        rows = nbuf[u].reshape(2 * tokens, wide)
        part = jnp.dot(rows, qwm[...], preferred_element_type=F32)
        pbuf[u, :, :, :, pl.ds(0, 2 * narrow)] = part.astype(BF16).reshape(4, 4, 16, 2 * narrow)
        for q in range(2):
            mate_copy(q, u).start()
        pl.when(t < UNITS - LOOK)(lambda: arrive(walk(t + LOOK)))

    def rel(q):
        return (z + 16 - 2 * (2 * c + x // 2) - q) % 8

    def z_copy(q, u):
        r = rel(q)
        far = r // 4
        at4 = (r == 4).astype(jnp.int32)
        down_way = at4 * (u % 2) + (1 - at4) * far
        to = (z + 8 + 2 * down_way - 1) % 8
        dev = (to % 2, tok, to // 2 * 2 + c)
        return remote(owned(q, u), zbuf.at[down_way, q, u], z_send.at[q], z_recv.at[down_way, q, u], dev)

    def z_wait(q, u, side):
        here = zbuf.at[side, q, u]
        remote(here, here, z_send.at[q], z_recv.at[side, q, u], mate).wait_recv()

    def fin_copy(q, u, local):
        one, two = offset(u % 4), offset(u // 4)
        to = ((x + one) % 4 * 4 + (y + two) % 4, (x + two) % 4 * 4 + (y + one) % 4)[q]
        dst = query.at[:, :, pl.ds(pl.multiple_of(y * narrow, narrow), narrow)]
        if local:
            return pltpu.make_async_copy(fin.at[u], dst, f_recv.at[y])
        return remote(fin.at[u], dst, f_send, f_recv.at[y], (zlo, to, zhi * 2 + x % 2))

    def relay(q, u):
        r = rel(q)
        here = owned(q, u)
        mate_copy(q, u).wait_recv()
        side = r // 4
        takes = jnp.logical_or(
            jnp.logical_or(r == 1, r == 2),
            jnp.logical_or(r >= 6, jnp.logical_or(
                jnp.logical_and(r == 3, u % 2 == 0), jnp.logical_and(r == 5, u % 2 == 1)
            )),
        )

        @pl.when(takes)
        def _():
            z_wait(q, u, side)
            here[...] = add(here[...], cbuf[q, u], zbuf[side, q, u]).astype(BF16)

        @pl.when(jnp.logical_and(jnp.logical_not(takes), r != 0))
        def _():
            here[...] = add(here[...], cbuf[q, u]).astype(BF16)

        @pl.when(r != 0)
        def _():
            z_copy(q, u).start()

        @pl.when(r == 0)
        def _():
            z_wait(q, u, 0)
            z_wait(q, u, 1)
            total = add(here[...], cbuf[q, u], zbuf[0, q, u], zbuf[1, q, u]).reshape(8, 16, narrow)
            fin[u] = (total + bias2[x % 2, y][0:1].reshape(1, 1, narrow)).astype(BF16)
            self_too = jnp.logical_and(u == 0, f_self)

            @pl.when(self_too)
            def _():
                fin_copy(q, u, True).start()

            @pl.when(jnp.logical_not(self_too))
            def _():
                fin_copy(q, u, False).start()

    def body2(t, carry):
        if EARLY:
            pl.when(t < UNITS)(lambda: multiply2(t))
        for q in range(2):
            r = rel(q)
            k = t - LAG1 - LAG2 * ((r - 4) * (2 * (r // 4) - 1))

            @pl.when(jnp.logical_and(k >= 0, k < UNITS))
            def _():
                relay(q, walk(k))

        if not EARLY:
            pl.when(t < UNITS)(lambda: multiply2(t))

        @pl.when(jnp.logical_and(t >= OUT_AT, t < OUT_AT + (8 if OUT_AT >= 0 else 0)))
        def _():
            for n in range(2):
                out_start(2 * (t - OUT_AT) + n)
        return carry

    lax.fori_loop(0, UNITS + LAG1 + 4 * LAG2, body2, 0)

    pltpu.make_async_copy(stream, stream, so_recv).wait()
    for n in range(4):
        dst = query.at[:, :, pl.ds(n * narrow, narrow)]
        pltpu.make_async_copy(dst, dst, f_recv.at[n]).wait()
    sent(stats.at[pl.ds(0, 15)], st_send)
    for q in range(2):
        sent(nbuf.at[pl.ds(0, 15), q], n_send.at[q])
        sent(cbuf.at[q], c_send.at[q])
        pl.when(rel(q) != 0)(lambda: sent(zbuf.at[0, q], z_send.at[q]))
    sent(rsrc.at[:, pl.ds(0, 15)], res_send.at[0])
    res_self = zhi // 2 == zlo
    pl.when(res_self)(lambda: sent(rbuf.at[pl.ds(0, 7)], res_send.at[1]))
    pl.when(jnp.logical_not(res_self))(lambda: sent(rbuf, res_send.at[1]))
    out_own = jnp.logical_and(zhi == 2 * zlo + x // 2, jnp.logical_and(c == x % 2, zlo == y // 2))
    pl.when(out_own)(lambda: sent(rsrc.at[:, pl.ds(0, 15)], so_send))
    pl.when(jnp.logical_not(out_own))(lambda: sent(rsrc, so_send))
    f_dest = zhi == 2 * c + x // 2
    pl.when(f_self)(lambda: sent(fin.at[pl.ds(0, 15)], f_send))
    pl.when(jnp.logical_and(f_dest, jnp.logical_not(f_self)))(lambda: sent(fin, f_send))


def per_device(
    hidden, resid, down_weight, down_bias, norm_gain, norm_shift, query_weight, query_bias
):
    rows, depth = hidden.shape
    width = down_weight.shape[1]
    wide = width // 2
    narrow = resid.shape[1]
    dma = pltpu.SemaphoreType.DMA
    vmem = pl.BlockSpec(memory_space=pltpu.VMEM)
    hbm = pl.BlockSpec(memory_space=pl.ANY)
    stream, query = pl.pallas_call(
        layer_kernel,
        out_shape=(
            jax.ShapeDtypeStruct((2, 16, 16, narrow), BF16),
            jax.ShapeDtypeStruct((8, 16, width), BF16),
        ),
        in_specs=[hbm, vmem, vmem, vmem, vmem, vmem, hbm, vmem],
        out_specs=(vmem, vmem),
        scratch_shapes=[
            pltpu.VMEM((8, 2, rows // 2, depth), BF16),
            pltpu.VMEM((2, 16, 16, narrow), BF16),
            pltpu.VMEM((16, 2, 16, narrow), BF16),
            pltpu.VMEM((8, 2, 2, 16, narrow), BF16),
            pltpu.VMEM((UNITS, 4, 4, 16, width), BF16),
            pltpu.VMEM((2, UNITS, 2, 2, 16, wide), BF16),
            pltpu.VMEM((2, UNITS, 2, 4, 16, wide), BF16),
            pltpu.VMEM((2, UNITS, 2, 16, wide // 2), BF16),
            pltpu.VMEM((2, UNITS, 2, 16, wide), BF16),
            pltpu.VMEM((UNITS, 16, wide), BF16),
            pltpu.VMEM((UNITS, 16, wide), BF16),
            pltpu.VMEM((2, 8, 16, wide), F32),
            pltpu.VMEM((2, 8, 16, wide), BF16),
            pltpu.VMEM((16, 2, 8, 128), F32),
            pltpu.VMEM((UNITS, 2, 128, wide), BF16),
            pltpu.VMEM((wide, 2 * narrow), BF16),
            pltpu.VMEM((2, 4, 8, narrow), F32),
            pltpu.VMEM((2, UNITS, 2, 4, 16, narrow), BF16),
            pltpu.VMEM((2, 2, UNITS, 2, 4, 16, narrow), BF16),
            pltpu.VMEM((UNITS, 8, 16, narrow), BF16),
            dma,
            dma((24,)),
            dma((16,)),
            dma((2,)),
            dma((2,)),
            dma((2, 5)),
            dma((UNITS, 2, 5, 2)),
            dma((3,)),
            dma((2,)),
            dma,
            dma((16,)),
            dma,
            dma,
            dma((2,)),
            dma((2, UNITS, 2)),
            dma((2,)),
            dma((2, UNITS)),
            dma((2,)),
            dma((2, 2, UNITS)),
            dma,
            dma((4,)),
        ],
        compiler_params=pltpu.CompilerParams(
            collective_id=0, has_side_effects=True, vmem_limit_bytes=62 * 1024 * 1024
        ),
        cost_estimate=pl.CostEstimate(
            flops=16 * rows * depth * width + 16 * rows * wide * wide,
            bytes_accessed=2 * (rows * depth + depth * width),
            transcendentals=0,
        ),
    )(
        hidden.reshape(2, rows // 2, depth),
        resid.reshape(2, 16, 16, narrow),
        down_bias,
        down_weight,
        norm_gain,
        norm_shift,
        query_weight.reshape(2, wide, narrow),
        query_bias,
    )
    return (stream.reshape(rows, narrow), query)


def solution(mesh):
    return jax.shard_map(
        per_device,
        mesh=mesh,
        in_specs=(
            P("wid", ST),
            P("wid", ST),
            P(ST, "wid"),
            P(ST),
            P("wid"),
            P("wid"),
            P("wid", ST),
            P("wid"),
        ),
        out_specs=(P("wid", ST), P(None, ST, "wid")),
        check_vma=False,
    )
```

```python
import functools

import jax
import jax.numpy as jnp
from jax import lax
from jax.experimental import pallas as pl
from jax.experimental.pallas import tpu as pltpu
from jax.sharding import PartitionSpec as P

norm_eps = 1e-05
ST = ("section", "tok")
F32, BF16 = jnp.float32, jnp.bfloat16
MESH = pl.DeviceIdType.MESH
UNITS = 16
LAG = 2
BEAT = 6
ORDER = (4, 3, 2, 1, 0)
LOOK = 1
WALK = (0, 1, 2, 4, 8, 5, 9, 6, 10, 3, 12, 7, 11, 13, 14, 15)
LAG1 = 1
LAG2 = 2
OUT_AT = -1
EARLY = False


def add(*terms):
    total = terms[0].astype(F32)
    for term in terms[1:]:
        total = total + term.astype(F32)
    return total


def place():
    zlo, tok, wid = (lax.axis_index(name) for name in ("section", "tok", "wid"))
    return zlo, tok // 4, tok % 4, wid // 2, wid % 2


def layer_kernel(
    hidden, resid, bias, weight, gain, shift, qweight, qbias, stream, query,
    hbuf, rsrc, rmid, rbuf, pbuf, r1, r2, r3, r4, zs, zr, acc,
    sbuf, stats, nbuf, qwm, bias2, cbuf, zbuf, fin,
    own_sem, ag_send, ag_recv, res_send, res_recv, rs_send, rs_recv,
    qw_sem, b_sem, st_send, st_recv, so_send, so_recv, n_send, n_recv,
    c_send, c_recv, z_send, z_recv, f_send, f_recv,
):
    zlo, x, y, zhi, c = place()
    tok, wid = x * 4 + y, zhi * 2 + c
    half = hbuf.shape[3]
    wide = weight.shape[1] // 2
    first, second = (x, y), (y, x)
    x_devs = [{"tok": (x + 1) % 4 * 4 + y}, {"tok": (x + 3) % 4 * 4 + y}]
    y_devs = [{"tok": x * 4 + (y + 1) % 4}, {"tok": x * 4 + (y + 3) % 4}]
    first_devs, second_devs = (x_devs, y_devs), (y_devs, x_devs)
    z_devs = [{"wid": (zhi + 1) % 4 * 2 + c}, {"wid": (zhi + 3) % 4 * 2 + c}]
    mate, pair = {"wid": zhi * 2 + 1 - c}, {"section": 1 - zlo}

    def remote(src, dst, send, recv, dev):
        return pltpu.make_async_remote_copy(src, dst, send, recv, device_id=dev, device_id_type=MESH)

    source = 4 * wid + 2 * zlo
    z = zhi * 2 + zlo
    me = z * 2 + c

    f_self = jnp.logical_and(zhi == 2 * c + x // 2, c == x % 2)

    barrier = pltpu.get_barrier_semaphore()

    def greet(dev):
        pl.semaphore_signal(barrier, inc=1, device_id=dev, device_id_type=MESH)

    for dev in (*x_devs, *y_devs):
        greet(dev)

    for dev in (*z_devs, mate, pair, {"section": 1 - zlo, "wid": (zhi + 3 + 2 * zlo) % 4 * 2 + c}):
        greet(dev)

    own_copy = pltpu.make_async_copy(hidden, hbuf.at[wid], own_sem)
    own_copy.start()
    narrow = resid.shape[3]
    place_at = pl.ds(pl.multiple_of((zlo + c) % 2 * narrow, narrow), narrow)
    qw_own = pltpu.make_async_copy(qweight.at[zlo], qwm.at[:, place_at], qw_sem.at[0])
    qw_own.start()
    rsrc[...] = (resid[...].astype(F32) + bias[...].reshape(1, 1, 1, -1)).astype(BF16)
    for n in range(4):
        bias2[c, n] = jnp.broadcast_to(qbias[n * narrow : (n + 1) * narrow].reshape(1, narrow), (8, narrow))
    pl.semaphore_wait(barrier, 4 + 5)

    def own_send(n):
        h = n % 2
        dev = (mate, *z_devs)[n // 2]
        step = (2 + h, 4 + 4 * h, 9 - 4 * h)[n // 2]
        return remote(hidden.at[h], hbuf.at[wid, h], ag_send.at[n], ag_recv.at[step], dev)

    for n in (2, 5, 0, 1):
        own_send(n).start()

    qw_pair = remote(qweight.at[1 - zlo], qwm.at[:, place_at], qw_sem.at[1], qw_sem.at[2], pair)
    bias_mate = remote(bias2.at[c], bias2.at[c], b_sem.at[0], b_sem.at[1], mate)
    bias_mate.start()

    def block(i):
        g, k = i // 4, i % 4
        mid = (g + 1) // 2 % 2
        off = mid * (3 - 2 * (k % 2)) + 2 * (g // 3)
        h = (k + mid * (g - 1)) % 2
        return (zhi + off) % 4 * 2 + (c + k // 2) % 2, h

    def mate_send(i):
        w, h = block(i)
        return remote(hbuf.at[w, h], hbuf.at[w, h], ag_send.at[8 + i], ag_recv.at[i + 2], mate)

    def far_send(i, n):
        w, h = block(i)
        return remote(hbuf.at[w, h], hbuf.at[w, h], ag_send.at[6 + n], ag_recv.at[12 + n], z_devs[n])

    def res_copy(n, local):
        src, dst = rsrc.at[:, n], rmid.at[tok]
        if local:
            return pltpu.make_async_copy(src, dst, res_recv.at[0])
        return remote(src, dst, res_send.at[0], res_recv.at[0], (zlo, n, wid))

    def res_start(n):
        pl.when(n == tok)(lambda: res_copy(n, True).start())
        pl.when(n != tok)(lambda: res_copy(n, False).start())

    def res_line(n, local):
        src, dst = rmid.at[pl.ds(2 * n, 2)], rbuf.at[wid]
        if local:
            return pltpu.make_async_copy(src, dst, res_recv.at[1])
        dev = (n % 2, tok, (zlo * 2 + n // 4) * 2 + n // 2 % 2)
        return remote(src, dst, res_send.at[1], res_recv.at[1], dev)

    def res_turn():
        sent(rmid, res_recv.at[0])
        for n in range(8):
            same = jnp.logical_and(
                n % 2 == zlo, jnp.logical_and(zlo * 2 + n // 4 == zhi, n // 2 % 2 == c)
            )
            pl.when(same)(lambda: res_line(n, True).start())
            pl.when(jnp.logical_not(same))(lambda: res_line(n, False).start())

    def sent(ref, sem):
        pltpu.make_async_copy(ref, ref, sem).wait()

    def chunk1(i, a, d, start, size):
        cols = pl.ds(a * wide, wide)
        if a == 0:
            return pbuf.at[i, d, pl.ds(start, size), :, cols]
        return pbuf.at[i, pl.ds(start, size), d, :, cols]

    def chunk2(i, a, d, start, size):
        cols = pl.ds(a * wide + start, size)
        if a == 0:
            return pbuf.at[i, x, d, :, cols]
        return pbuf.at[i, d, y, :, cols]

    def hop(i, a, s, n):
        sems = rs_send.at[a, s], rs_recv.at[i, a, s, n]
        near = (1, 3)[n]
        if s == 0:
            return remote(chunk1(i, a, (first[a] + 2) % 4, 2 * n, 2), r1.at[a, i, n], *sems, first_devs[a][n])
        if s == 1:
            return remote(chunk1(i, a, (first[a] + near) % 4, 0, 4), r2.at[a, i, n], *sems, first_devs[a][n])
        if s == 2:
            src = chunk2(i, a, (second[a] + 2) % 4, n * wide // 2, wide // 2)
            return remote(src, r3.at[a, i, n], *sems, second_devs[a][n])
        return remote(chunk2(i, a, (second[a] + near) % 4, 0, wide), r4.at[a, i, n], *sems, second_devs[a][n])

    def pair_hop(i):
        return remote(zs.at[i], zr.at[i], rs_send.at[0, 4], rs_recv.at[i, 0, 4, 0], pair)

    def multiply(i):
        w, h = block(i)

        @pl.when(i == 0)
        def _():
            own_copy.wait()

        for step, gone, then in ((4, (2, 5), (own_send(3), own_send(4))), (8, (3, 4), (far_send(4, 0), far_send(5, 1)))):
            @pl.when(i == step)
            def _():
                for n, copy in zip(gone, then):
                    own_send(n).wait_send()
                    copy.start()

        @pl.when(i >= 2)
        def _():
            remote(hbuf.at[w, h], hbuf.at[w, h], ag_send.at[0], ag_recv.at[i], mate).wait_recv()

        @pl.when(jnp.logical_and(i >= 4, i % 4 < 2))
        def _():
            mate_send(i).start()

        pl.when(i == 10)(res_turn)
        pl.when(i == 8)(qw_pair.start)

        rows = hbuf[w, h]
        for n in range(0, 2 * wide, 512):
            part = jnp.dot(rows, weight[:, n : n + 512], preferred_element_type=F32)
            pbuf[i, :, :, :, pl.ds(n, 512)] = part.astype(BF16).reshape(4, 4, 16, 512)
        for a in range(2):
            for n in range(2):
                hop(i, a, 0, n).start()

    def relay1(i):
        for a in range(2):
            for n in range(2):
                hop(i, a, 0, n).wait_recv()
                ref = chunk1(i, a, (first[a] + (1, 3)[n]) % 4, 2 * n, 2)
                ref[...] = add(ref[...], r1[a, i, n]).astype(BF16)
                hop(i, a, 1, n).start()

    def turn(i):
        for a in range(2):
            for n in range(2):
                hop(i, a, 1, n).wait_recv()
            ref = chunk1(i, a, first[a], 0, 4)
            ref[...] = add(ref[...], r2[a, i, 0], r2[a, i, 1]).astype(BF16)
            for n in range(2):
                hop(i, a, 2, n).start()

    def relay2(i):
        for a in range(2):
            for n in range(2):
                hop(i, a, 2, n).wait_recv()
                ref = chunk2(i, a, (second[a] + (1, 3)[n]) % 4, n * wide // 2, wide // 2)
                ref[...] = add(ref[...], r3[a, i, n]).astype(BF16)
                hop(i, a, 3, n).start()

    def plane_sum(i):
        for a in range(2):
            for n in range(2):
                hop(i, a, 3, n).wait_recv()
            total = add(chunk2(i, a, second[a], 0, wide)[...], r4[a, i, 0], r4[a, i, 1])

            @pl.when(zlo == a)
            def _():
                w, h = block(i)
                acc[h, w] = total

            @pl.when(zlo != a)
            def _():
                zs[i] = total.astype(BF16)
                pair_hop(i).start()

    def finish(i):
        w, h = block(i)
        pair_hop(i).wait_recv()
        acc[h, w] = add(acc[h, w], zr[i])

    stages = (multiply, relay1, turn, relay2, plane_sum)

    def body(t, carry):
        for n in ORDER:
            turn_at = t - n * LAG
            i = turn_at // BEAT * 4 + turn_at % BEAT
            due = jnp.logical_and(turn_at % BEAT < 4, i < UNITS)

            @pl.when(jnp.logical_and(turn_at >= 0, due))
            def _():
                stages[n](i)

        @pl.when(jnp.logical_and(t > 4 * LAG, t < 4 * LAG + 5))
        def _():
            for n in range(4):
                res_start(4 * (t - 4 * LAG - 1) + n)

        end = 3 * BEAT + 4 * LAG

        @pl.when(t >= end)
        def _():
            for n in range(3):
                finish(3 * (t - end) + n)
        return carry

    lax.fori_loop(0, 3 * BEAT + 4 + 4 * LAG, body, 0)

    def finish_each(i, carry):
        finish(i)
        return carry

    lax.fori_loop(12, UNITS, finish_each, 0)

    sent(rbuf, res_recv.at[1])
    for q in range(2):
        for n in range(2):
            cols = pl.ds(n * narrow, narrow)
            sbuf[q, :, :, cols] = add(acc[q, :, :, cols], rbuf[:, n, q]).astype(BF16)

    tokens = sbuf.shape[1] * sbuf.shape[2]
    lane = lax.broadcasted_iota(jnp.int32, (tokens, tokens), 1)
    row = lax.broadcasted_iota(jnp.int32, (tokens, tokens), 0)
    for q in range(2):
        values = sbuf[q].reshape(tokens, wide).astype(F32)
        mean = jnp.mean(values, axis=1, keepdims=True)
        m2 = jnp.sum((values - mean) ** 2, axis=1, keepdims=True)
        stats[me, q] = jnp.where(lane == 0, mean, m2).T[:8]

    def stat_copy(n):
        dev = (n // 2 % 2, tok, n // 4 * 2 + n % 2)
        return remote(stats.at[me], stats.at[me], st_send, st_recv.at[me], dev)

    def others(action):
        def step(n, carry):
            pl.when(n != me)(lambda: action(n))
            return carry

        lax.fori_loop(0, 16, step, 0)

    others(lambda n: stat_copy(n).start())

    def out_copy(n, local):
        group = source + n // 8
        src = sbuf.at[:, n % 8, :, pl.ds(pl.multiple_of(n // 8 * narrow, narrow), narrow)]
        dst = stream.at[:, tok]
        if local:
            return pltpu.make_async_copy(src, dst, so_recv)
        return remote(src, dst, so_send, so_recv, (group // 16, group % 16, n % 8))

    def out_self(n):
        return jnp.logical_and(source + n // 8 == zlo * 16 + tok, n % 8 == wid)

    def out_start(n):
        pl.when(out_self(n))(lambda: out_copy(n, True).start())
        pl.when(jnp.logical_not(out_self(n)))(lambda: out_copy(n, False).start())

    for n in range(2):
        own_send(n).wait_send()
    for i in (4, 5, 8, 9, 12, 13):
        mate_send(i).wait_send()
    far_send(4, 0).wait_send()
    far_send(5, 1).wait_send()

    for a in range(2):
        for n, ref in enumerate((r1, r2, r3, r4)):
            sent(ref.at[a], rs_send.at[a, n])
    sent(zr, rs_send.at[0, 4])

    if OUT_AT < 0:
        def out_each(n, carry):
            out_start(n)
            return carry

        lax.fori_loop(0, 16, out_each, 0)

    def stat_wait(n):
        here = stats.at[n]
        remote(here, here, st_send, st_recv.at[n], mate).wait_recv()

    others(stat_wait)
    gains, shifts = (
        jnp.where(zlo == 0, ref[0:wide], ref[wide : 2 * wide]).reshape(1, wide) for ref in (gain, shift)
    )
    for q in range(2):
        means, m2s = stats[:, q, 0, :], stats[:, q, 1, :]
        mean = jnp.mean(means, axis=0, keepdims=True)
        var = jnp.sum(m2s, axis=0, keepdims=True) + wide * jnp.sum((means - mean) ** 2, axis=0, keepdims=True)
        scale = lax.rsqrt(var / (16 * wide) + norm_eps)
        both = jnp.where(row == 0, mean, scale).T
        values = sbuf[q].reshape(tokens, wide).astype(F32)
        normed = (values - both[:, 0:1]) * both[:, 1:2] * gains + shifts
        nbuf[0, q] = normed.astype(BF16)

    mid = tokens // 2

    def pass_on(q, u, to, dev, part=None):
        if part is None:
            src, dst = nbuf.at[u, q], nbuf.at[to, q]
        else:
            rows = pl.ds(part * mid, mid)
            src, dst = nbuf.at[u, q, rows], nbuf.at[to, q, rows]
        return remote(src, dst, n_send.at[q], n_recv.at[q, to, part or 0], dev)

    def passes(q, u):
        (fp, fm), (sp, sm) = first_devs[q], second_devs[q]
        return (
            (u == 0, lambda: pass_on(q, u, 1, fp)),
            (u == 0, lambda: pass_on(q, u, 2, fm)),
            (u == 1, lambda: pass_on(q, u, 3, fp, 0)),
            (u == 2, lambda: pass_on(q, u, 3, fm, 1)),
            (u < 4, lambda: pass_on(q, u, 4 + u, sp)),
            (u < 4, lambda: pass_on(q, u, 8 + u, sm)),
            (u // 4 == 1, lambda: pass_on(q, u, 8 + u, sp, 0)),
            (u // 4 == 2, lambda: pass_on(q, u, 4 + u, sm, 1)),
        )

    def offset(e):
        return 3 * e + 3 * (e // 2) + 2 * (e // 3)

    def owned(q, u):
        return pbuf.at[u, pl.ds(2 * q, 2), :, :, pl.ds(0, narrow)]

    def given(q, u):
        return pbuf.at[u, pl.ds(2 * q, 2), :, :, pl.ds(narrow, narrow)]

    def mate_copy(q, u):
        return remote(given(q, u), cbuf.at[q, u], c_send.at[q], c_recv.at[q, u], mate)

    def walk(k):
        return sum((k == n).astype(jnp.int32) * u for n, u in enumerate(WALK))

    def arrive(u):
        for q in range(2):
            split = jnp.logical_or(u == 3, u >= 12)

            @pl.when(jnp.logical_and(u > 0, jnp.logical_not(split)))
            def _():
                here = nbuf.at[u, q]
                remote(here, here, n_send.at[q], n_recv.at[q, u, 0], mate).wait_recv()

            @pl.when(split)
            def _():
                for part in range(2):
                    here = nbuf.at[u, q, pl.ds(part * mid, mid)]
                    remote(here, here, n_send.at[q], n_recv.at[q, u, part], mate).wait_recv()

            for cond, copy in passes(q, u):
                @pl.when(cond)
                def _():
                    copy().start()

    def multiply2(t):
        @pl.when(t == 0)
        def _():
            arrive(0 * t)
            for n in range(1, LOOK):
                arrive(walk(n + 0 * t))

        u = walk(t)

        @pl.when(t == 0)
        def _():
            qw_own.wait()
            qw_pair.wait()
            bias_mate.wait()

        rows = nbuf[u].reshape(2 * tokens, wide)
        part = jnp.dot(rows, qwm[...], preferred_element_type=F32)
        pbuf[u, :, :, :, pl.ds(0, 2 * narrow)] = part.astype(BF16).reshape(4, 4, 16, 2 * narrow)
        for q in range(2):
            mate_copy(q, u).start()
        pl.when(t < UNITS - LOOK)(lambda: arrive(walk(t + LOOK)))

    def rel(q):
        return (z + 16 - 2 * (2 * c + x // 2) - q) % 8

    def z_copy(q, u):
        r = rel(q)
        far = r // 4
        at4 = (r == 4).astype(jnp.int32)
        down_way = at4 * (u % 2) + (1 - at4) * far
        to = (z + 8 + 2 * down_way - 1) % 8
        dev = (to % 2, tok, to // 2 * 2 + c)
        return remote(owned(q, u), zbuf.at[down_way, q, u], z_send.at[q], z_recv.at[down_way, q, u], dev)

    def z_wait(q, u, side):
        here = zbuf.at[side, q, u]
        remote(here, here, z_send.at[q], z_recv.at[side, q, u], mate).wait_recv()

    def fin_copy(q, u, local):
        one, two = offset(u % 4), offset(u // 4)
        to = ((x + one) % 4 * 4 + (y + two) % 4, (x + two) % 4 * 4 + (y + one) % 4)[q]
        dst = query.at[:, :, pl.ds(pl.multiple_of(y * narrow, narrow), narrow)]
        if local:
            return pltpu.make_async_copy(fin.at[u], dst, f_recv.at[y])
        return remote(fin.at[u], dst, f_send, f_recv.at[y], (zlo, to, zhi * 2 + x % 2))

    def relay(q, u):
        r = rel(q)
        here = owned(q, u)
        mate_copy(q, u).wait_recv()
        side = r // 4
        takes = jnp.logical_or(
            jnp.logical_or(r == 1, r == 2),
            jnp.logical_or(r >= 6, jnp.logical_or(
                jnp.logical_and(r == 3, u % 2 == 0), jnp.logical_and(r == 5, u % 2 == 1)
            )),
        )

        @pl.when(takes)
        def _():
            z_wait(q, u, side)
            here[...] = add(here[...], cbuf[q, u], zbuf[side, q, u]).astype(BF16)

        @pl.when(jnp.logical_and(jnp.logical_not(takes), r != 0))
        def _():
            here[...] = add(here[...], cbuf[q, u]).astype(BF16)

        @pl.when(r != 0)
        def _():
            z_copy(q, u).start()

        @pl.when(r == 0)
        def _():
            z_wait(q, u, 0)
            z_wait(q, u, 1)
            total = add(here[...], cbuf[q, u], zbuf[0, q, u], zbuf[1, q, u]).reshape(8, 16, narrow)
            fin[u] = (total + bias2[x % 2, y][0:1].reshape(1, 1, narrow)).astype(BF16)
            self_too = jnp.logical_and(u == 0, f_self)

            @pl.when(self_too)
            def _():
                fin_copy(q, u, True).start()

            @pl.when(jnp.logical_not(self_too))
            def _():
                fin_copy(q, u, False).start()

    def body2(t, carry):
        if EARLY:
            pl.when(t < UNITS)(lambda: multiply2(t))
        for q in range(2):
            r = rel(q)
            k = t - LAG1 - LAG2 * ((r - 4) * (2 * (r // 4) - 1))

            @pl.when(jnp.logical_and(k >= 0, k < UNITS))
            def _():
                relay(q, walk(k))

        if not EARLY:
            pl.when(t < UNITS)(lambda: multiply2(t))

        @pl.when(jnp.logical_and(t >= OUT_AT, t < OUT_AT + (8 if OUT_AT >= 0 else 0)))
        def _():
            for n in range(2):
                out_start(2 * (t - OUT_AT) + n)
        return carry

    lax.fori_loop(0, UNITS + LAG1 + 4 * LAG2, body2, 0)

    pltpu.make_async_copy(stream, stream, so_recv).wait()
    for n in range(4):
        dst = query.at[:, :, pl.ds(n * narrow, narrow)]
        pltpu.make_async_copy(dst, dst, f_recv.at[n]).wait()
    sent(stats.at[pl.ds(0, 15)], st_send)
    for q in range(2):
        sent(nbuf.at[pl.ds(0, 15), q], n_send.at[q])
        sent(cbuf.at[q], c_send.at[q])
        pl.when(rel(q) != 0)(lambda: sent(zbuf.at[0, q], z_send.at[q]))
    sent(rsrc.at[:, pl.ds(0, 15)], res_send.at[0])
    res_self = zhi // 2 == zlo
    pl.when(res_self)(lambda: sent(rbuf.at[pl.ds(0, 7)], res_send.at[1]))
    pl.when(jnp.logical_not(res_self))(lambda: sent(rbuf, res_send.at[1]))
    out_own = jnp.logical_and(zhi == 2 * zlo + x // 2, jnp.logical_and(c == x % 2, zlo == y // 2))
    pl.when(out_own)(lambda: sent(rsrc.at[:, pl.ds(0, 15)], so_send))
    pl.when(jnp.logical_not(out_own))(lambda: sent(rsrc, so_send))
    f_dest = zhi == 2 * c + x // 2
    pl.when(f_self)(lambda: sent(fin.at[pl.ds(0, 15)], f_send))
    pl.when(jnp.logical_and(f_dest, jnp.logical_not(f_self)))(lambda: sent(fin, f_send))


def per_device(
    hidden, resid, down_weight, down_bias, norm_gain, norm_shift, query_weight, query_bias
):
    rows, depth = hidden.shape
    width = down_weight.shape[1]
    wide = width // 2
    narrow = resid.shape[1]
    dma = pltpu.SemaphoreType.DMA
    vmem = pl.BlockSpec(memory_space=pltpu.VMEM)
    hbm = pl.BlockSpec(memory_space=pl.ANY)
    stream, query = pl.pallas_call(
        layer_kernel,
        out_shape=(
            jax.ShapeDtypeStruct((2, 16, 16, narrow), BF16),
            jax.ShapeDtypeStruct((8, 16, width), BF16),
        ),
        in_specs=[hbm, vmem, vmem, vmem, vmem, vmem, hbm, vmem],
        out_specs=(vmem, vmem),
        scratch_shapes=[
            pltpu.VMEM((8, 2, rows // 2, depth), BF16),
            pltpu.VMEM((2, 16, 16, narrow), BF16),
            pltpu.VMEM((16, 2, 16, narrow), BF16),
            pltpu.VMEM((8, 2, 2, 16, narrow), BF16),
            pltpu.VMEM((UNITS, 4, 4, 16, width), BF16),
            pltpu.VMEM((2, UNITS, 2, 2, 16, wide), BF16),
            pltpu.VMEM((2, UNITS, 2, 4, 16, wide), BF16),
            pltpu.VMEM((2, UNITS, 2, 16, wide // 2), BF16),
            pltpu.VMEM((2, UNITS, 2, 16, wide), BF16),
            pltpu.VMEM((UNITS, 16, wide), BF16),
            pltpu.VMEM((UNITS, 16, wide), BF16),
            pltpu.VMEM((2, 8, 16, wide), F32),
            pltpu.VMEM((2, 8, 16, wide), BF16),
            pltpu.VMEM((16, 2, 8, 128), F32),
            pltpu.VMEM((UNITS, 2, 128, wide), BF16),
            pltpu.VMEM((wide, 2 * narrow), BF16),
            pltpu.VMEM((2, 4, 8, narrow), F32),
            pltpu.VMEM((2, UNITS, 2, 4, 16, narrow), BF16),
            pltpu.VMEM((2, 2, UNITS, 2, 4, 16, narrow), BF16),
            pltpu.VMEM((UNITS, 8, 16, narrow), BF16),
            dma,
            dma((24,)),
            dma((16,)),
            dma((2,)),
            dma((2,)),
            dma((2, 5)),
            dma((UNITS, 2, 5, 2)),
            dma((3,)),
            dma((2,)),
            dma,
            dma((16,)),
            dma,
            dma,
            dma((2,)),
            dma((2, UNITS, 2)),
            dma((2,)),
            dma((2, UNITS)),
            dma((2,)),
            dma((2, 2, UNITS)),
            dma,
            dma((4,)),
        ],
        compiler_params=pltpu.CompilerParams(
            collective_id=0, has_side_effects=True, vmem_limit_bytes=62 * 1024 * 1024
        ),
        cost_estimate=pl.CostEstimate(
            flops=16 * rows * depth * width + 16 * rows * wide * wide,
            bytes_accessed=2 * (rows * depth + depth * width),
            transcendentals=0,
        ),
    )(
        hidden.reshape(2, rows // 2, depth),
        resid.reshape(2, 16, 16, narrow),
        down_bias,
        down_weight,
        norm_gain,
        norm_shift,
        query_weight.reshape(2, wide, narrow),
        query_bias,
    )
    return (stream.reshape(rows, narrow), query)


def solution(mesh):
    return jax.shard_map(
        per_device,
        mesh=mesh,
        in_specs=(
            P("wid", ST),
            P("wid", ST),
            P(ST, "wid"),
            P(ST),
            P("wid"),
            P("wid"),
            P("wid", ST),
            P("wid"),
        ),
        out_specs=(P("wid", ST), P(None, ST, "wid")),
        check_vma=False,
    )
```
